128 devices in a mesh: row: 4 (over z), col: 32 (over x, y, core).
Axes of the slice: x: 4, y: 4, z: 4, core: 2. Of those that a mesh axis runs over, the one named last changes fastest.
Arguments:
- features: bfloat16 [49152, 128], P(('row', 'col')), may hold values from -6 to 6
- weight: bfloat16 [128, 128], replicated, may hold values from -0.5 to 0.5
- tiles: bfloat16 [4, 8192, 128, 128], P('row', 'col'), may hold values from -0.09375 to 0.09375
- tile_dest: int32 [4, 8192], P('row', 'col'), may hold values from 0 to 95, as said below
- tile_src: int32 [4, 8192], P('row', 'col'), may hold values from 0 to 11, as said below
- tile_count: int32 [4, 32], P('row', 'col'), may hold values from 32 to 256, as said below
- source_of: int32 [49152], P(('row', 'col')), may hold values from 0 to 49151, as said below
- out_grad: bfloat16 [49152, 128], P(('row', 'col')), may hold values from -6 to 6
Outputs:
- activations: bfloat16 [49152, 128], P(('row', 'col'))
- feature_grad: bfloat16 [49152, 128], P(('row', 'col'))
- weight_grad: float32 [128, 128], replicated
The draws below stay inside these ranges and needn't reach their ends.
Inputs may be any that keep to these rules, and one draw needn't show every extreme that they name: `tile_dest`: the slots of one device name distinct tiles. `tile_src`: the slots of one device name distinct tiles. `tile_count`: some device has all of its 256 slots live. `source_of`: a permutation of the 49152 vertices; of the 384 destination positions of each device, exactly 3 hold source vertices of each device.
All inputs are finite; a program needn't handle non-finite values.
Results may differ from the reference program's by a relative error of at most 0.017.
Values may be sent and summed in bfloat16 or wider, within the bound.
A program may use at most 64 MiB of HBM per device.

```python
import math
import jax
import jax.numpy as jnp
from jax import lax

WIDTH = 128
TILE = 128
ROWS_DEV = 384
TILES_DEV = 256
STRIPS = 4
COLUMNS = 32
GROUPS = 128
NODES = 49152
PAIR = 3
STRIP_BLOCKS = 96
GROUP_BLOCKS = 12
SLOTS = 8192
N_COL = 32


def tile_layout(key):
    key_cells = jax.random.fold_in(key, 11)
    grid_size = STRIP_BLOCKS * GROUP_BLOCKS
    key_list = jax.random.split(key_cells, GROUPS)
    chosen = jax.vmap(lambda subkey: jax.random.permutation(subkey, grid_size)[:TILES_DEV])(key_list)
    return chosen.reshape(STRIPS, SLOTS).astype(jnp.int32)


def draw_tile_dest(key, part):
    return (tile_layout(key) // GROUP_BLOCKS).astype(jnp.int32)


def draw_tile_src(key, part):
    return (tile_layout(key) % GROUP_BLOCKS).astype(jnp.int32)


def draw_tile_count(key, part):
    key_load = jax.random.fold_in(key, 12)
    raw_load = jax.random.randint(key_load, (GROUPS,), 0, TILES_DEV + 1)
    loads = jnp.maximum(TILES_DEV // 8, raw_load * raw_load // TILES_DEV)
    full_device = jax.random.randint(jax.random.fold_in(key_load, 1), (), 0, GROUPS)
    loads = jnp.where(jnp.arange(GROUPS) == full_device, TILES_DEV, loads)
    return loads.reshape(STRIPS, COLUMNS).astype(jnp.int32)


def draw_source_of(key, part):
    key_send = jax.random.fold_in(key, 21)
    key_place = jax.random.fold_in(key, 22)
    local_perm = jax.vmap(lambda subkey: jax.random.permutation(subkey, ROWS_DEV))(jax.random.split(key_send, GROUPS))
    vertex = local_perm + jnp.arange(GROUPS)[:, None] * ROWS_DEV
    vertex = vertex.reshape(GROUPS, GROUPS, PAIR).transpose(1, 0, 2).reshape(GROUPS, ROWS_DEV)
    shuffle = jax.vmap(lambda subkey: jax.random.permutation(subkey, ROWS_DEV))(jax.random.split(key_place, GROUPS))
    placed = jnp.take_along_axis(vertex, shuffle, axis=1)
    return placed.reshape(NODES).astype(jnp.int32)


def block_scale(rng, shape, shards, least, high):
    loudness = 1.0
    for axis_at, blocks in shards:
        draws = jax.random.uniform(jax.random.fold_in(jax.random.fold_in(rng, 6), axis_at), (blocks,), jnp.float32, least / len(shards), high / len(shards))
        loudness = loudness * jnp.repeat(jnp.exp(draws), shape[axis_at] // blocks).reshape((-1,) + (1,) * (len(shape) - 1 - axis_at))
    return loudness


def scatter_about(own_key, extent, scale, reach, shards=(), kind=jnp.bfloat16):
    drawn = scale * jax.random.normal(own_key, extent, jnp.float32)
    if shards:
        drawn = drawn * block_scale(own_key, extent, shards, -0.22, 0.18)
    return jnp.clip(drawn, -reach, reach).astype(kind)


def setup_inputs(seed: int = 0) -> dict:
    key_of = jax.random.split(jax.random.key(seed), 9)
    features = scatter_about(key_of[0], (NODES, WIDTH), 1.0, 6.0, ((0, 128),))
    weight = scatter_about(key_of[1], (WIDTH, WIDTH), WIDTH ** -0.5, 0.5)
    tiles = scatter_about(key_of[2], (STRIPS, SLOTS, TILE, TILE), (max(TILE, TILE * TILES_DEV * N_COL // (3 * STRIP_BLOCKS))) ** -0.5, 0.09375, ((0, 4), (1, 32)))
    tile_dest = draw_tile_dest(jax.random.fold_in(key_of[8], 71), 0)
    tile_src = draw_tile_src(jax.random.fold_in(key_of[8], 71), 0)
    tile_count = draw_tile_count(jax.random.fold_in(key_of[8], 71), 0)
    source_of = draw_source_of(jax.random.fold_in(key_of[8], 71), 0)
    out_grad = scatter_about(key_of[7], (NODES, WIDTH), 1.0, 6.0, ((0, 128),))
    return dict(features=features, weight=weight, tiles=tiles, tile_dest=tile_dest, tile_src=tile_src, tile_count=tile_count, source_of=source_of, out_grad=out_grad)


def silu_slope(values):
    sigma = jax.nn.sigmoid(values)
    return sigma * (1.0 + values * (1.0 - sigma))

def reference(features, weight, tiles, tile_dest, tile_src, tile_count, source_of, out_grad):
    hidden = jnp.dot(features, weight, preferred_element_type=jnp.float32).astype(jnp.bfloat16)
    group_rows = hidden.reshape(STRIPS, COLUMNS, ROWS_DEV, WIDTH).transpose(1, 0, 2, 3)
    group_rows = group_rows.reshape(COLUMNS, GROUP_BLOCKS, TILE, WIDTH)
    tile_sets = tiles.reshape(GROUPS, TILES_DEV, TILE, TILE)
    dest_sets = tile_dest.reshape(GROUPS, TILES_DEV)
    source_sets = tile_src.reshape(GROUPS, TILES_DEV)
    load_sets = tile_count.reshape(GROUPS)
    devices = jnp.arange(GROUPS, dtype=jnp.int32)

    def forward_step(totals, device):
        strip_idx = device // COLUMNS
        col_idx = device % COLUMNS
        operand = group_rows[col_idx][source_sets[device]]
        product = jnp.einsum('bij,bjf->bif', tile_sets[device].astype(jnp.float32), operand.astype(jnp.float32))
        live_mask = jnp.arange(TILES_DEV) < load_sets[device]
        product = jnp.where(live_mask[:, None, None], product, 0.0)
        return (totals.at[strip_idx, dest_sets[device]].add(product), None)
    start_sums = jnp.zeros((STRIPS, STRIP_BLOCKS, TILE, WIDTH), jnp.float32)
    strip_sums, _ = lax.scan(forward_step, start_sums, devices)
    pre = strip_sums.reshape(NODES, WIDTH).astype(jnp.bfloat16)
    pre_float = pre.astype(jnp.float32)
    act_dest = jax.nn.silu(pre_float).astype(jnp.bfloat16)
    activations = jnp.zeros((NODES, WIDTH), jnp.bfloat16).at[source_of].set(act_dest)
    dest_grad = out_grad[source_of].astype(jnp.float32)
    pre_grad = (dest_grad * silu_slope(pre_float)).astype(jnp.bfloat16)
    strip_grad = pre_grad.reshape(STRIPS, STRIP_BLOCKS, TILE, WIDTH)

    def backward_step(totals, device):
        strip_idx = device // COLUMNS
        col_idx = device % COLUMNS
        operand = strip_grad[strip_idx][dest_sets[device]]
        product = jnp.einsum('bji,bjf->bif', tile_sets[device].astype(jnp.float32), operand.astype(jnp.float32))
        live_mask = jnp.arange(TILES_DEV) < load_sets[device]
        product = jnp.where(live_mask[:, None, None], product, 0.0)
        return (totals.at[col_idx, source_sets[device]].add(product), None)
    start_grads = jnp.zeros((COLUMNS, GROUP_BLOCKS, TILE, WIDTH), jnp.float32)
    group_grads, _ = lax.scan(backward_step, start_grads, devices)
    hidden_grad = group_grads.reshape(COLUMNS, STRIPS, ROWS_DEV, WIDTH).transpose(1, 0, 2, 3)
    hidden_grad = hidden_grad.reshape(NODES, WIDTH).astype(jnp.bfloat16)
    feature_grad = jnp.dot(hidden_grad, weight.T, preferred_element_type=jnp.float32).astype(jnp.bfloat16)
    weight_grad = jnp.dot(features.T, hidden_grad, preferred_element_type=jnp.float32) / math.sqrt(NODES)
    return (activations, feature_grad, weight_grad)
```

```python
import functools
import math

import jax
import jax.numpy as jnp
from jax import lax
from jax.experimental import pallas as pl
from jax.experimental.pallas import tpu as pltpu
from jax.sharding import PartitionSpec as P

MESH = pl.DeviceIdType.MESH
F32 = jnp.float32
BF16 = jnp.bfloat16
UNROLL = 8


def mm(a, b):
    return jnp.dot(a, b, preferred_element_type=F32)


def sigmoid(v):
    return 1.0 / (1.0 + jnp.exp(-v))


def iota(shape, dim):
    return lax.broadcasted_iota(jnp.int32, shape, dim)


def kernel(
    dest_s, src_s, prevd_s, prevs_s, lastd_s, lasts_s,
    feat, weight, tiles_hbm, slot_row, slot_col, id_rows, out_grad,
    act_out, fg_out, wg_out,
    tiles, run, fall, hid,
    place, place_t, regroup, regroup_t, pick, pick_t,
    id_m, id_z, id_g, id_c,
    og_m, og_c, og_g, og_z,
    ac_m, ac_z, ac_g, ac_c,
    sib_out, sib_in, x_out, y_out, x_in, y_in, x2_out, y2_out, x2_in, y2_in,
    dgrad, gath, hg_out, hg_in, hgt, dw, dw_in, dw_col, dw_colin, dw_sum, dw_all, dw_full,
    t_sem, sig,
    f_s, f_r, idz_s, idz_r, idc_s, idc_r, ogc_s, ogc_r, ogz_s, ogz_r, acz_s, acz_r, acc_s, acc_r,
    sib_s, sib_r, rx_s, rx_r, ry_s, ry_r, rx2_s, rx2_r, ry2_s, ry2_r,
    ax_s, ax_r, ay_s, ay_r, ax2_s, ax2_r, ay2_s, ay2_r, as_s, as_r,
    hg_s, hg_r, wz_s, wz_r, wc_s, wc_r, wg_s, wg_r, wa_s, wa_r,
):
    r = lax.axis_index("row")
    c = lax.axis_index("col")
    x = c // 8
    y = (c // 2) % 4
    e = c % 2
    sibling = x * 8 + y * 2 + (1 - e)

    def send(src, dst, ss, rs, row, col):
        cp = pltpu.make_async_remote_copy(
            src_ref=src, dst_ref=dst, send_sem=ss, recv_sem=rs,
            device_id={"row": row, "col": col}, device_id_type=MESH)
        cp.start()
        return cp

    def arrived(view, sem):
        pltpu.make_async_copy(view, view, sem).wait()

    def to_rows(src_of, dst, ss, rs):
        out = []
        for d in range(1, 4):
            to = lax.rem(r + d, 4)
            out.append(send(src_of(to), dst.at[r], ss.at[d - 1], rs.at[d - 1], to, c))
        return out

    def to_cols(src, dst, ss, rs):
        def one(d, carry):
            to = lax.rem(c + d, 32)
            send(src.at[to], dst.at[c], ss, rs, r, to)
            return carry
        lax.fori_loop(1, 32, one, 0)

    def cols_done(src, dst, ss, rs):
        arrived(src.at[pl.ds(0, 31)], ss)
        arrived(dst.at[pl.ds(0, 31)], rs)

    def done(copies):
        for cp in copies:
            cp.wait()

    barrier = pltpu.get_barrier_semaphore()

    def greet(d, carry):
        pl.semaphore_signal(barrier, inc=1, device_id={"row": r, "col": lax.rem(c + d, 32)}, device_id_type=MESH)
        return carry
    lax.fori_loop(1, 32, greet, 0)
    for d in range(1, 4):
        pl.semaphore_signal(barrier, inc=1, device_id={"row": lax.rem(r + d, 4), "col": c}, device_id_type=MESH)
    loads = [pltpu.make_async_copy(tiles_hbm.at[pl.ds(64 * k, 64)], tiles.at[pl.ds(64 * k, 64)], t_sem.at[k]) for k in range(4)]
    for cp in loads:
        cp.start()

    place[...] = jnp.where(iota((384, 384), 0) == slot_row[...], 1.0, 0.0).astype(BF16)
    place_t[...] = jnp.where(slot_col[...] == iota((384, 384), 1), 1.0, 0.0).astype(BF16)
    q = iota((512, 384), 0)
    s = iota((512, 384), 1)
    regroup[...] = jnp.where(((q & 3) < 3) & (s == ((q >> 2) & 3) * 96 + (q >> 4) * 3 + (q & 3)), 1.0, 0.0).astype(BF16)
    q = iota((384, 512), 1)
    s = iota((384, 512), 0)
    regroup_t[...] = jnp.where(((q & 3) < 3) & (s == ((q >> 2) & 3) * 96 + (q >> 4) * 3 + (q & 3)), 1.0, 0.0).astype(BF16)
    run[256] = jnp.zeros((128, 128), F32)
    id_m[...] = mm(place[...], id_rows[...]).astype(BF16).reshape(4, 96, 128)
    fall[r] = feat[...]
    pl.semaphore_wait(barrier, 34)

    f_copies = to_rows(lambda to: feat, fall, f_s, f_r)
    idz = to_rows(lambda to: id_m.at[to], id_z, idz_s, idz_r)
    id_z[r] = id_m[r]
    done(f_copies)
    hid[...] = mm(fall[...].reshape(1536, 128), weight[...]).astype(BF16).reshape(12, 128, 128)
    done(idz)
    id_g[...] = mm(regroup[...], id_z[...].reshape(384, 128)).astype(BF16).reshape(32, 16, 128)
    to_cols(id_g, id_c, idc_s, idc_r)
    id_c[c] = id_g[c]

    for cp in loads:
        cp.wait()

    def forward(i, carry):
        for k in range(UNROLL):
            t = i * UNROLL + k
            run[t] = run[prevd_s[t]] + mm(tiles[t], hid[src_s[t]])
        return carry
    lax.fori_loop(0, 256 // UNROLL, forward, 0)

    sib = []
    for g in range(4):
        def fill(k, carry, g=g):
            chip = g * 4 + k
            for j in range(3):
                b = (chip * 2 + (1 - e)) * 3 + j
                sib_out[chip, pl.ds(j * 128, 128), :] = run[lastd_s[b]].astype(BF16)
            return carry
        lax.fori_loop(0, 4, fill, 0)
        part = pl.ds(g * 4, 4)
        sib.append(send(sib_out.at[part], sib_in.at[part], sib_s.at[g], sib_r.at[g], r, sibling))

    cols_done(id_g, id_c, idc_s, idc_r)
    numbers = id_c[...].reshape(512, 128).astype(F32)
    col_id = (2.0 * numbers[:, 0:1] + numbers[:, 64:65]).astype(jnp.int32)
    pick[...] = jnp.where((col_id == iota((512, 384), 1)) & ((iota((512, 384), 0) & 3) < 3), 1.0, 0.0).astype(BF16)
    flipped = numbers.T
    row_id = (2.0 * flipped[0:1, :] + flipped[64:65, :]).astype(jnp.int32)
    pick_t[...] = jnp.where((row_id == iota((384, 512), 0)) & ((iota((384, 512), 1) & 3) < 3), 1.0, 0.0).astype(BF16)
    og_m[...] = mm(pick[...], out_grad[...]).astype(BF16).reshape(32, 16, 128)
    to_cols(og_m, og_c, ogc_s, ogc_r)
    og_c[c] = og_m[c]

    for g in range(4):
        sib[g].wait_recv()

        def both(k, carry, g=g):
            chip = g * 4 + k
            b = (chip * 2 + e) * 3
            rows0 = run[lastd_s[b]]
            rows1 = run[lastd_s[b + 1]]
            rows2 = run[lastd_s[b + 2]]
            got = sib_in[chip].astype(F32)
            x_out[g, k, pl.ds(0, 128), :] = (rows0 + got[0:128]).astype(BF16)
            x_out[g, k, pl.ds(128, 64), :] = (rows1[0:64] + got[128:192]).astype(BF16)
            y_out[k, g, pl.ds(0, 64), :] = (rows1[64:128] + got[192:256]).astype(BF16)
            y_out[k, g, pl.ds(64, 128), :] = (rows2 + got[256:384]).astype(BF16)
            return carry
        lax.fori_loop(0, 4, both, 0)
    for g in range(4):
        sib[g].wait_send()

    def at_chip(px, py):
        return px * 8 + py * 2 + e

    rx, ry = [], []
    for d in (2, 1, 3):
        px = lax.rem(x + d, 4)
        rx.append(send(x_out.at[px], x_in.at[x], rx_s.at[d - 1], rx_r.at[d - 1], r, at_chip(px, y)))
        py = lax.rem(y + d, 4)
        ry.append(send(y_out.at[py], y_in.at[y], ry_s.at[d - 1], ry_r.at[d - 1], r, at_chip(x, py)))

    cols_done(og_m, og_c, ogc_s, ogc_r)
    og_g[...] = mm(regroup_t[...], og_c[...].reshape(512, 128)).astype(BF16).reshape(4, 96, 128)
    ogz = to_rows(lambda to: og_g.at[to], og_z, ogz_s, ogz_r)
    og_z[r] = og_g[r]

    done(rx)

    def sum_x(k, carry):
        total = x_out[x, k].astype(F32)
        for d in range(1, 4):
            total += x_in[lax.rem(x + d, 4), k].astype(F32)
        x2_out[k] = total.astype(BF16)
        return carry
    lax.fori_loop(0, 4, sum_x, 0)
    rx2 = []
    for d in (2, 1, 3):
        py = lax.rem(y + d, 4)
        rx2.append(send(x2_out.at[py], x2_in.at[y], rx2_s.at[d - 1], rx2_r.at[d - 1], r, at_chip(x, py)))
    done(ry)

    def sum_y(k, carry):
        total = y_out[y, k].astype(F32)
        for d in range(1, 4):
            total += y_in[lax.rem(y + d, 4), k].astype(F32)
        y2_out[k] = total.astype(BF16)
        return carry
    lax.fori_loop(0, 4, sum_y, 0)
    ry2 = []
    for d in (2, 1, 3):
        px = lax.rem(x + d, 4)
        ry2.append(send(y2_out.at[px], y2_in.at[x], ry2_s.at[d - 1], ry2_r.at[d - 1], r, at_chip(px, y)))

    done(ogz)
    dgrad[...] = mm(place_t[...], og_z[...].reshape(384, 128))

    done(rx2)
    top = x2_out[y].astype(F32)
    for d in range(1, 4):
        top += x2_in[lax.rem(y + d, 4)].astype(F32)
    done(ry2)
    low = y2_out[x].astype(F32)
    for d in range(1, 4):
        low += y2_in[lax.rem(x + d, 4)].astype(F32)
    pre = jnp.concatenate([top, low], axis=0).astype(BF16).astype(F32)
    sg = sigmoid(pre)
    grad = (dgrad[...] * (sg * (1.0 + pre * (1.0 - sg)))).astype(BF16).astype(F32)
    for j in range(3):
        block = grad[j * 128:(j + 1) * 128].T.astype(BF16)
        if j == 0:
            gath[x, y, e, 0, pl.ds(0, 128), :] = block
        elif j == 1:
            gath[x, y, e, 0, pl.ds(128, 64), :] = block[0:64]
            gath[x, y, e, 1, pl.ds(0, 64), :] = block[64:128]
        else:
            gath[x, y, e, 1, pl.ds(64, 128), :] = block

    ax, ay = [], []
    for d in (2, 1, 3):
        part = gath.at[x, y, e, 0]
        ax.append(send(part, part, ax_s.at[d - 1], ax_r.at[d - 1], r, at_chip(lax.rem(x + d, 4), y)))
        part = gath.at[x, y, e, 1]
        ay.append(send(part, part, ay_s.at[d - 1], ay_r.at[d - 1], r, at_chip(x, lax.rem(y + d, 4))))
    act_rows = (pre * sg).astype(BF16)
    ac_m[...] = mm(place[...], act_rows).astype(BF16).reshape(4, 96, 128)
    acz = to_rows(lambda to: ac_m.at[to], ac_z, acz_s, acz_r)
    ac_z[r] = ac_m[r]

    done(ax)
    ax2, ay2, asib = [], [], []
    for d in (2, 1, 3):
        part = gath.at[:, y, e, 0]
        ax2.append(send(part, part, ax2_s.at[d - 1], ax2_r.at[d - 1], r, at_chip(x, lax.rem(y + d, 4))))
    done(ay)
    for d in (2, 1, 3):
        part = gath.at[x, :, e, 1]
        ay2.append(send(part, part, ay2_s.at[d - 1], ay2_r.at[d - 1], r, at_chip(lax.rem(x + d, 4), y)))
    part = gath.at[:, y, e, 0]
    asib.append(send(part, part, as_s.at[0], as_r.at[0], r, sibling))
    part = gath.at[x, :, e, 1]
    asib.append(send(part, part, as_s.at[1], as_r.at[1], r, sibling))

    done(acz)
    ac_g[...] = mm(regroup[...], ac_z[...].reshape(384, 128)).astype(BF16).reshape(32, 16, 128)
    to_cols(ac_g, ac_c, acc_s, acc_r)
    ac_c[c] = ac_g[c]

    order = (2, 1, 3)
    for n in (1, 2, 0):
        d = order[n]
        ax2[n].wait_recv()
        part = gath.at[:, lax.rem(y - d + 4, 4), e, 0]
        asib.append(send(part, part, as_s.at[1 + d], as_r.at[1 + d], r, sibling))
        ay2[n].wait_recv()
        part = gath.at[lax.rem(x - d + 4, 4), :, e, 1]
        asib.append(send(part, part, as_s.at[4 + d], as_r.at[4 + d], r, sibling))

    cols_done(ac_g, ac_c, acc_s, acc_r)
    act_out[...] = mm(pick_t[...], ac_c[...].reshape(512, 128)).astype(BF16)

    for n in range(3):
        ax2[n].wait_send()
        ay2[n].wait_send()
    done(asib)

    def backward(i, carry):
        for k in range(UNROLL):
            t = i * UNROLL + k
            b = dest_s[t]
            owner = b // 3
            j = b - owner * 3
            g = grads[b]
            run[t] = run[prevs_s[t]] + mm(g, tiles[t])
        return carry
    grads = gath.reshape(96, 128, 128)
    lax.fori_loop(0, 256 // UNROLL, backward, 0)

    def finish(k, carry):
        hg_out[k] = run[lasts_s[k]].astype(BF16)
        return carry
    lax.fori_loop(0, 12, finish, 0)
    hgc = []
    for d in (2, 1, 3):
        to = lax.rem(r + d, 4)
        hgc.append(send(hg_out.at[pl.ds(to * 3, 3)], hg_in.at[r], hg_s.at[d - 1], hg_r.at[d - 1], to, c))

    dwt = jnp.zeros((128, 128), F32)
    for k in range(12):
        dwt += mm(hg_out[k], fall[k // 3, pl.ds((k % 3) * 128, 128), :])
    dw[...] = dwt.T.reshape(4, 32, 128)
    wz = to_rows(lambda to: dw.at[to], dw_in, wz_s, wz_r)
    done(wz)
    total = dw[r]
    for d in range(1, 4):
        total += dw_in[lax.rem(r + d, 4)]
    dw_col[...] = total.reshape(32, 1, 128)
    to_cols(dw_col, dw_colin, wc_s, wc_r)
    dw_colin[c] = dw_col[c]

    done(hgc)
    for j in range(3):
        part = hg_out[r * 3 + j].astype(F32)
        for d in range(1, 4):
            part += hg_in[lax.rem(r + d, 4), j].astype(F32)
        fg_out[pl.ds(j * 128, 128), :] = mm(weight[...], part.astype(BF16)).T.astype(BF16)

    cols_done(dw_col, dw_colin, wc_s, wc_r)
    mine = jnp.sum(dw_colin[...].reshape(32, 128), axis=0, keepdims=True) * (1.0 / math.sqrt(49152.0))
    dw_sum[...] = jnp.broadcast_to(mine.reshape(1, 1, 128), (32, 1, 128))
    to_cols(dw_sum, dw_all, wg_s, wg_r)
    dw_all[c] = dw_sum[c]
    cols_done(dw_sum, dw_all, wg_s, wg_r)
    dw_full[r] = dw_all[...].reshape(32, 128)
    wa = []
    for d in (2, 1, 3):
        to = lax.rem(r + d, 4)
        wa.append(send(dw_full.at[r], dw_full.at[r], wa_s.at[d - 1], wa_r.at[d - 1], to, c))
    done(wa)
    wg_out[...] = dw_full[...].reshape(128, 128)


def local(features, weight, tiles, tile_dest, tile_src, tile_count, source_of, out_grad):
    dest, src, live = tile_dest[0], tile_src[0], tile_count[0, 0]
    at = jnp.arange(256, dtype=jnp.int32)

    def previous(key):
        same = (key[:, None] == key[None, :]) & (at[None, :] < at[:, None])
        return jnp.max(jnp.where(same, at[None, :] + 1, 0), axis=1)

    def last(key, count):
        same = (key[None, :] == jnp.arange(count, dtype=jnp.int32)[:, None]) & (at[None, :] < live)
        return jnp.max(jnp.where(same, at[None, :] + 1, 0), axis=1)

    def slot(v):
        return jnp.where(v == 0, 256, v - 1)

    owner = source_of // 384
    place = jnp.arange(384, dtype=jnp.int32)
    rank = jnp.sum(((owner[:, None] == owner[None, :]) & (place[None, :] < place[:, None])).astype(jnp.int32), axis=1)
    spot = owner * 3 + rank
    number = source_of - owner * 384
    id_rows = jnp.where(jnp.arange(128)[None, :] < 64, (number >> 1)[:, None], (number & 1)[:, None]).astype(BF16)

    def V(*shape, dtype=BF16):
        return pltpu.VMEM(shape, dtype)

    def D(n=None):
        return pltpu.SemaphoreType.DMA((n,)) if n else pltpu.SemaphoreType.DMA

    scratch = [
        V(256, 128, 128), V(257, 128, 128, dtype=F32), V(4, 384, 128), V(12, 128, 128),
        V(384, 384), V(384, 384), V(512, 384), V(384, 512), V(512, 384), V(384, 512),
        V(4, 96, 128), V(4, 96, 128), V(32, 16, 128), V(32, 16, 128),
        V(32, 16, 128), V(32, 16, 128), V(4, 96, 128), V(4, 96, 128),
        V(4, 96, 128), V(4, 96, 128), V(32, 16, 128), V(32, 16, 128),
        V(16, 384, 128), V(16, 384, 128), V(4, 4, 192, 128), V(4, 4, 192, 128), V(4, 4, 192, 128), V(4, 4, 192, 128),
        V(4, 192, 128), V(4, 192, 128), V(4, 192, 128), V(4, 192, 128),
        V(384, 128, dtype=F32), V(4, 4, 2, 2, 192, 128), V(12, 128, 128), V(4, 3, 128, 128), V(3, 128, 128),
        V(4, 32, 128, dtype=F32), V(4, 32, 128, dtype=F32), V(32, 1, 128, dtype=F32), V(32, 1, 128, dtype=F32),
        V(32, 1, 128, dtype=F32), V(32, 1, 128, dtype=F32), V(4, 32, 128, dtype=F32),
        D(4), D(),
        D(3), D(3), D(3), D(3), D(), D(), D(), D(), D(3), D(3), D(3), D(3), D(), D(),
        D(4), D(4), D(3), D(3), D(3), D(3), D(3), D(3), D(3), D(3),
        D(3), D(3), D(3), D(3), D(3), D(3), D(3), D(3), D(8), D(8),
        D(3), D(3), D(3), D(3), D(), D(), D(), D(), D(3), D(3),
    ]
    smem = pl.BlockSpec(memory_space=pltpu.SMEM)
    vmem = pl.BlockSpec(memory_space=pltpu.VMEM)
    return pl.pallas_call(
        kernel,
        out_shape=(
            jax.ShapeDtypeStruct((384, 128), BF16),
            jax.ShapeDtypeStruct((384, 128), BF16),
            jax.ShapeDtypeStruct((128, 128), F32),
        ),
        in_specs=[smem] * 6 + [vmem, vmem, pl.BlockSpec(memory_space=pl.ANY)] + [vmem] * 4,
        out_specs=(vmem, vmem, vmem),
        scratch_shapes=scratch,
        compiler_params=pltpu.CompilerParams(
            collective_id=0, has_side_effects=True, vmem_limit_bytes=56 * 2**20),
    )(
        dest, src, slot(previous(dest)), slot(previous(src)), slot(last(dest, 96)), slot(last(src, 12)),
        features, weight, tiles[0], spot[None, :], spot[:, None], id_rows, out_grad,
    )


def solution(mesh):
    placed = (
        P(("row", "col"), None),
        P(),
        P("row", "col", None, None),
        P("row", "col"),
        P("row", "col"),
        P("row", "col"),
        P(("row", "col")),
        P(("row", "col"), None),
    )
    return jax.shard_map(
        local,
        mesh=mesh,
        in_specs=placed,
        out_specs=(P(("row", "col"), None), P(("row", "col"), None), P()),
        check_vma=False,
    )
```

```python
import functools
import math

import jax
import jax.numpy as jnp
from jax import lax
from jax.experimental import pallas as pl
from jax.experimental.pallas import tpu as pltpu
from jax.sharding import PartitionSpec as P

MESH = pl.DeviceIdType.MESH
F32 = jnp.float32
BF16 = jnp.bfloat16
UNROLL = 32


def mm(a, b):
    return jnp.dot(a, b, preferred_element_type=F32)


def sigmoid(v):
    return 1.0 / (1.0 + jnp.exp(-v))


def iota(shape, dim):
    return lax.broadcasted_iota(jnp.int32, shape, dim)


def kernel(
    dest_h, src_h, count_s, owner_h, feat_h, weight_h, grad_h, tiles_h,
    act_out, fg_out, wg_out,
    tiles, run, fall, weight, out_grad, dest_v, src_v, owner_v,
    dest_s, src_s, prevd_v, prevs_v, lastd_v, lasts_v, prevd_s, prevs_s, lastd_s, lasts_s,
    place, place_t, regroup, regroup_t, pick, pick_t,
    id_m, id_z, id_g, id_c,
    og_m, og_c, og_g, og_z,
    ac_m, ac_z, ac_g, ac_c,
    sx_out, sy_out, sx_in, sy_in, x_out, y_out, x_in, y_in, x2_out, y2_out, x2_in, y2_in,
    dgrad, gath, hg_out, hg_in, dw, dw_in, dw_col, dw_colin, dw_sum, dw_all, dw_full,
    l_sem, t_sem, i_sem,
    f_s, f_r, idz_s, idz_r, idc_s, idc_r, ogc_s, ogc_r, ogz_s, ogz_r, acz_s, acz_r, acc_s, acc_r,
    sx_s, sx_r, sy_s, sy_r, rx_s, rx_r, ry_s, ry_r, rx2_s, rx2_r, ry2_s, ry2_r,
    ax_s, ax_r, ay_s, ay_r, gx_s, gx_r, gy_s, gy_r, as_s, as_r,
    hg_s, hg_r, wz_s, wz_r, wc_s, wc_r, wg_s, wg_r, wa_s, wa_r,
):
    r = lax.axis_index("row")
    c = lax.axis_index("col")
    x = c // 8
    y = (c // 2) % 4
    e = c % 2

    def at_chip(px, py):
        return {"row": r, "col": px * 8 + py * 2 + e}

    sibling = {"row": r, "col": x * 8 + y * 2 + (1 - e)}

    def send(src, dst, ss, rs, device):
        cp = pltpu.make_async_remote_copy(
            src_ref=src, dst_ref=dst, send_sem=ss, recv_sem=rs,
            device_id=device, device_id_type=MESH)
        cp.start()
        return cp

    def arrived(view, sem):
        pltpu.make_async_copy(view, view, sem).wait()

    def to_rows(src_of, dst, ss, rs):
        out = []
        for d in (2, 1, 3):
            to = lax.rem(r + d, 4)
            out.append(send(src_of(to), dst.at[r], ss.at[d - 1], rs.at[d - 1], {"row": to, "col": c}))
        return out

    def to_cols(src, dst, ss, rs):
        def one(d, carry):
            to = lax.rem(c + d, 32)
            send(src.at[to], dst.at[c], ss, rs, {"row": r, "col": to})
            return carry
        lax.fori_loop(1, 32, one, 0)

    def cols_done(src, dst, ss, rs):
        arrived(src.at[pl.ds(0, 31)], ss)
        arrived(dst.at[pl.ds(0, 31)], rs)

    def done(copies):
        for cp in copies:
            cp.wait()

    class Gather:
        def __init__(self, view, me, device, ss, rs):
            self.view, self.ss, self.rs = view, ss, rs
            self.right, self.left = lax.rem(me + 1, 4), lax.rem(me + 3, 4)
            self.to_right, self.to_left = device(self.right), device(self.left)
            self.copies = {}
            for n, half, device in ((0, 0, self.to_right), (2, 1, self.to_left), (1, 1, self.to_right), (3, 0, self.to_left)):
                self.go(n, view(me, half), device)

        def go(self, n, ref, device):
            self.copies[n] = send(ref, ref, self.ss.at[n], self.rs.at[n], device)

        def relay(self):
            self.copies[0].wait_recv()
            self.go(4, self.view(self.left, 0), self.to_right)
            self.copies[2].wait_recv()
            self.go(5, self.view(self.right, 1), self.to_left)

        def near(self):
            self.copies[1].wait_recv()
            self.copies[3].wait_recv()

        def far(self):
            self.copies[4].wait_recv()
            self.copies[5].wait_recv()

        def sent(self):
            for n in range(6):
                self.copies[n].wait_send()

    class Reduce:
        def __init__(self, out, into, half, me, device, ss, rs):
            self.out, self.into, self.half, self.me = out, into, half, me
            self.ss, self.rs = ss, rs
            self.right, self.left = lax.rem(me + 1, 4), lax.rem(me + 3, 4)
            self.across = lax.rem(me + 2, 4)
            self.to_right, self.to_left = device(self.right), device(self.left)
            self.copies = {}

        def go(self, n, pos, half, device):
            self.copies[n] = send(
                self.out.at[(pos,) + self.half(half)], self.into.at[n], self.ss.at[n], self.rs.at[n], device)

        def send_across(self):
            self.go(0, self.across, 0, self.to_right)
            self.go(2, self.across, 1, self.to_left)

        def send_right(self):
            self.go(1, self.right, 1, self.to_right)

        def send_left(self):
            self.go(3, self.left, 0, self.to_left)

        def relay(self):
            for n, pos, half, device in ((0, self.right, 0, self.to_right), (2, self.left, 1, self.to_left)):
                self.copies[n].wait_recv()
                at = (pos,) + self.half(half)
                self.out[at] = (self.out[at].astype(F32) + self.into[n].astype(F32)).astype(BF16)
                self.go(4 + n // 2, pos, half, device)

        def total(self, half):
            first, second = ((3, 4), (1, 5))[half]
            self.copies[first].wait_recv()
            own = self.out[(self.me,) + self.half(half)].astype(F32) + self.into[first].astype(F32)
            self.copies[second].wait_recv()
            return own + self.into[second].astype(F32)

        def sent(self):
            for n in range(6):
                self.copies[n].wait_send()

    barrier = pltpu.get_barrier_semaphore()

    def greet(d, carry):
        pl.semaphore_signal(barrier, inc=1, device_id={"row": r, "col": lax.rem(c + d, 32)}, device_id_type=MESH)
        return carry
    lax.fori_loop(1, 32, greet, 0)
    for d in range(1, 4):
        pl.semaphore_signal(barrier, inc=1, device_id={"row": lax.rem(r + d, 4), "col": c}, device_id_type=MESH)

    def load(n, src, dst):
        cp = pltpu.make_async_copy(src, dst, l_sem.at[n])
        cp.start()
        return cp

    feat_load = load(0, feat_h, fall.at[r])
    key_loads = [load(1, dest_h, dest_v), load(2, src_h, src_v), load(3, owner_h, owner_v)]
    scalar_loads = [load(4, dest_h, dest_s), load(5, src_h, src_s)]
    later_loads = [load(6, weight_h, weight), load(7, grad_h, out_grad)]
    tile_loads = [pltpu.make_async_copy(tiles_h.at[pl.ds(64 * k, 64)], tiles.at[pl.ds(64 * k, 64)], t_sem.at[k]) for k in range(4)]
    for cp in tile_loads:
        cp.start()
    feat_load.wait()
    pl.semaphore_wait(barrier, 34)

    half_rows = (pl.ds(0, 192), pl.ds(192, 192))
    features = Gather(lambda pos, half: fall.at[pos, half_rows[half]], r, lambda pos: {"row": pos, "col": c}, f_s, f_r)
    done(key_loads)

    source_of = owner_v[...].reshape(1, 384).astype(F32)
    owner = jnp.floor((source_of + 0.5) * (1.0 / 384.0))
    number = source_of - owner * 384.0
    owner_all = jnp.broadcast_to(owner, (384, 384))
    earlier = (owner_all.T == owner_all) & (iota((384, 384), 0) < iota((384, 384), 1))
    rank = jnp.sum(jnp.where(earlier, 1.0, 0.0), axis=0, keepdims=True)
    spot = owner * 3.0 + rank
    spots = jnp.where(iota((384, 384), 0).astype(F32) == spot, 1.0, 0.0)
    place[...] = spots.astype(BF16)
    sent_id = jnp.sum(spots * number, axis=1, keepdims=True)
    upper = jnp.floor(sent_id * 0.5)
    id_m[...] = jnp.where(iota((384, 128), 1) < 64, upper, sent_id - 2.0 * upper).astype(BF16).reshape(4, 96, 128)
    idz = to_rows(lambda to: id_m.at[to], id_z, idz_s, idz_r)
    id_z[r] = id_m[r]

    live = count_s[0, 0]

    def chains(key_v, prev_v, last_v, prev_s, last_s, n):
        key = jnp.broadcast_to(key_v[...], (256, 256))
        flipped = key.T
        at = iota((256, 256), 0)
        before = jnp.where((flipped == key) & (at < iota((256, 256), 1)), at, -1)
        best = jnp.max(before, axis=0, keepdims=True)
        prev_v[...] = jnp.where(best < 0, 256, best)
        at = iota((256, 128), 0)
        named = jnp.where((flipped[:, 0:128] == iota((256, 128), 1)) & (at < live), at, -1)
        best = jnp.max(named, axis=0, keepdims=True)
        last_v[...] = jnp.where(best < 0, 256, best)
        return [pltpu.make_async_copy(prev_v, prev_s, i_sem.at[n]), pltpu.make_async_copy(last_v, last_s, i_sem.at[n + 1])]

    index_loads = chains(dest_v, prevd_v, lastd_v, prevd_s, lastd_s, 0) + chains(src_v, prevs_v, lasts_v, prevs_s, lasts_s, 2)
    for cp in index_loads:
        cp.start()

    features.relay()
    run[256] = jnp.zeros((128, 128), F32)
    q = iota((512, 384), 0)
    s = iota((512, 384), 1)
    spread = jnp.where(((q & 3) < 3) & (s == ((q >> 2) & 3) * 96 + (q >> 4) * 3 + (q & 3)), 1.0, 0.0)
    regroup[...] = spread.astype(BF16)
    regroup_t[...] = spread.T.astype(BF16)
    place_t[...] = spots.T.astype(BF16)
    done(idz)
    id_g[...] = mm(regroup[...], id_z[...].reshape(384, 128)).astype(BF16).reshape(32, 16, 128)
    to_cols(id_g, id_c, idc_s, idc_r)
    id_c[c] = id_g[c]
    done(index_loads)
    done(scalar_loads)
    done(tile_loads)
    features.near()
    features.far()

    blocks = fall.reshape(12, 128, 128)

    def forward(i, carry):
        for k in range(UNROLL):
            t = i * UNROLL + k
            run[t] = run[prevd_s[0, t]] + mm(tiles[t], blocks[src_s[0, t]])
        return carry
    lax.fori_loop(0, 256 // UNROLL, forward, 0)

    steps = (("x", 2), ("y", 2), ("x", 1), ("x", 3), ("y", 1), ("y", 3), ("x", 0), ("y", 0))

    def first_rows(chip, core):
        b = (chip * 2 + core) * 3
        return run[lastd_s[0, b]], run[lastd_s[0, b + 1], pl.ds(0, 64), :]

    def last_rows(chip, core):
        b = (chip * 2 + core) * 3
        return run[lastd_s[0, b + 1], pl.ds(64, 64), :], run[lastd_s[0, b + 2]]

    sib = {}
    for axis, d in steps:
        if axis == "x":
            g = lax.rem(x + d, 4)
            for k in range(4):
                rows0, rows1 = first_rows(g * 4 + k, 1 - e)
                sx_out[g, k, pl.ds(0, 128), :] = rows0.astype(BF16)
                sx_out[g, k, pl.ds(128, 64), :] = rows1.astype(BF16)
            sib[axis, d] = send(sx_out.at[g], sx_in.at[g], sx_s.at[d], sx_r.at[d], sibling)
        else:
            g = lax.rem(y + d, 4)
            for k in range(4):
                rows0, rows1 = last_rows(k * 4 + g, 1 - e)
                sy_out[g, k, pl.ds(0, 64), :] = rows0.astype(BF16)
                sy_out[g, k, pl.ds(64, 128), :] = rows1.astype(BF16)
            sib[axis, d] = send(sy_out.at[g], sy_in.at[g], sy_s.at[d], sy_r.at[d], sibling)

    def pair(half):
        return (pl.ds(2 * half, 2),)

    rx = Reduce(x_out, x_in, pair, x, lambda pos: at_chip(pos, y), rx_s, rx_r)
    ry = Reduce(y_out, y_in, pair, y, lambda pos: at_chip(x, pos), ry_s, ry_r)
    for axis, d in steps:
        sib[axis, d].wait_recv()
        if axis == "x":
            g = lax.rem(x + d, 4)
            for k in range(4):
                rows0, rows1 = first_rows(g * 4 + k, e)
                x_out[g, k, pl.ds(0, 128), :] = (rows0 + sx_in[g, k, pl.ds(0, 128), :].astype(F32)).astype(BF16)
                x_out[g, k, pl.ds(128, 64), :] = (rows1 + sx_in[g, k, pl.ds(128, 64), :].astype(F32)).astype(BF16)
        else:
            g = lax.rem(y + d, 4)
            for k in range(4):
                rows0, rows1 = last_rows(k * 4 + g, e)
                y_out[g, k, pl.ds(0, 64), :] = (rows0 + sy_in[g, k, pl.ds(0, 64), :].astype(F32)).astype(BF16)
                y_out[g, k, pl.ds(64, 128), :] = (rows1 + sy_in[g, k, pl.ds(64, 128), :].astype(F32)).astype(BF16)
        ring = rx if axis == "x" else ry
        if d == 2:
            ring.send_across()
        elif d == 1:
            ring.send_right()
        elif d == 3:
            ring.send_left()

    done(later_loads)
    cols_done(id_g, id_c, idc_s, idc_r)
    numbers = id_c[...].reshape(512, 128).astype(F32)
    slot_id = 2.0 * numbers[:, 0:1] + numbers[:, 64:65]
    picked = jnp.where((slot_id == iota((512, 384), 1).astype(F32)) & ((iota((512, 384), 0) & 3) < 3), 1.0, 0.0)
    pick[...] = picked.astype(BF16)
    og_m[...] = mm(pick[...], out_grad[...]).astype(BF16).reshape(32, 16, 128)
    to_cols(og_m, og_c, ogc_s, ogc_r)
    og_c[c] = og_m[c]

    rx.relay()
    ry.relay()
    pick_t[...] = picked.T.astype(BF16)
    cols_done(og_m, og_c, ogc_s, ogc_r)
    og_g[...] = mm(regroup_t[...], og_c[...].reshape(512, 128)).astype(BF16).reshape(4, 96, 128)
    ogz = to_rows(lambda to: og_g.at[to], og_z, ogz_s, ogz_r)
    og_z[r] = og_g[r]

    rx2, ry2 = [], []
    for half in range(2):
        x2_out[pl.ds(2 * half, 2)] = rx.total(half).astype(BF16)
    for d in (2, 1, 3):
        py = lax.rem(y + d, 4)
        rx2.append(send(x2_out.at[py], x2_in.at[y], rx2_s.at[d - 1], rx2_r.at[d - 1], at_chip(x, py)))
    for half in range(2):
        y2_out[pl.ds(2 * half, 2)] = ry.total(half).astype(BF16)
    for d in (2, 1, 3):
        px = lax.rem(x + d, 4)
        ry2.append(send(y2_out.at[px], y2_in.at[x], ry2_s.at[d - 1], ry2_r.at[d - 1], at_chip(px, y)))

    done(ogz)
    dgrad[...] = mm(place_t[...], og_z[...].reshape(384, 128))
    rx.sent()
    ry.sent()
    for step in steps:
        sib[step].wait_send()
    features.sent()

    done(rx2)
    top = x2_out[y].astype(F32)
    for d in range(1, 4):
        top += x2_in[lax.rem(y + d, 4)].astype(F32)
    done(ry2)
    low = y2_out[x].astype(F32)
    for d in range(1, 4):
        low += y2_in[lax.rem(x + d, 4)].astype(F32)
    sums = jnp.concatenate([top, low], axis=0)
    sums_high = sums.astype(BF16)
    sums_low = (sums - sums_high.astype(F32)).astype(BF16)
    pre = (mm(sums_high, weight[...]) + mm(sums_low, weight[...])).astype(BF16).astype(F32)
    sg = sigmoid(pre)
    grad = (dgrad[...] * (sg * (1.0 + pre * (1.0 - sg)))).astype(BF16).astype(F32)
    turned = [grad[j * 128:(j + 1) * 128].T.astype(BF16) for j in range(3)]
    gath[x, y, e, 0, pl.ds(0, 128), :] = turned[0]
    gath[x, y, e, 0, pl.ds(128, 64), :] = turned[1][0:64]
    gath[x, y, e, 1, pl.ds(0, 64), :] = turned[1][64:128]
    gath[x, y, e, 1, pl.ds(64, 128), :] = turned[2]

    ax, ay = [], []
    for d in (2, 1, 3):
        part = gath.at[x, y, e, 0]
        ax.append(send(part, part, ax_s.at[d - 1], ax_r.at[d - 1], at_chip(lax.rem(x + d, 4), y)))
        part = gath.at[x, y, e, 1]
        ay.append(send(part, part, ay_s.at[d - 1], ay_r.at[d - 1], at_chip(x, lax.rem(y + d, 4))))

    ac_m[...] = mm(place[...], (pre * sg).astype(BF16)).astype(BF16).reshape(4, 96, 128)
    acz = to_rows(lambda to: ac_m.at[to], ac_z, acz_s, acz_r)
    ac_z[r] = ac_m[r]
    term = jnp.zeros((128, 128), F32)
    for j in range(3):
        rows = slice(j * 128, (j + 1) * 128)
        term += mm(turned[j], sums_high[rows]) + mm(turned[j], sums_low[rows])
    dw[...] = term.T.reshape(4, 32, 128)
    wz = to_rows(lambda to: dw.at[to], dw_in, wz_s, wz_r)

    done(ax)
    by_y = Gather(lambda pos, half: gath.at[pl.ds(2 * half, 2), pos, e, 0], y, lambda pos: at_chip(x, pos), gy_s, gy_r)
    done(ay)
    by_x = Gather(lambda pos, half: gath.at[pos, pl.ds(2 * half, 2), e, 1], x, lambda pos: at_chip(pos, y), gx_s, gx_r)
    asib = []

    def share(n, part):
        asib.append(send(part, part, as_s.at[n], as_r.at[n], sibling))

    share(0, gath.at[:, y, e, 0])
    share(1, gath.at[x, :, e, 1])

    done(acz)
    ac_g[...] = mm(regroup[...], ac_z[...].reshape(384, 128)).astype(BF16).reshape(32, 16, 128)
    to_cols(ac_g, ac_c, acc_s, acc_r)
    ac_c[c] = ac_g[c]

    by_y.relay()
    by_x.relay()
    by_y.near()
    share(2, gath.at[:, by_y.left, e, 0])
    share(3, gath.at[:, by_y.right, e, 0])
    by_x.near()
    share(4, gath.at[by_x.left, :, e, 1])
    share(5, gath.at[by_x.right, :, e, 1])

    done(wz)
    total = dw[r]
    for d in range(1, 4):
        total += dw_in[lax.rem(r + d, 4)]
    dw_col[...] = total.reshape(32, 1, 128)
    to_cols(dw_col, dw_colin, wc_s, wc_r)
    dw_colin[c] = dw_col[c]

    by_y.far()
    share(6, gath.at[:, lax.rem(y + 2, 4), e, 0])
    by_x.far()
    share(7, gath.at[lax.rem(x + 2, 4), :, e, 1])

    cols_done(ac_g, ac_c, acc_s, acc_r)
    act_out[...] = mm(pick_t[...], ac_c[...].reshape(512, 128)).astype(BF16)
    by_y.sent()
    by_x.sent()
    done(asib)

    grads = gath.reshape(96, 128, 128)

    def backward(i, carry):
        for k in range(UNROLL):
            t = i * UNROLL + k
            run[t] = run[prevs_s[0, t]] + mm(grads[dest_s[0, t]], tiles[t])
        return carry
    lax.fori_loop(0, 128 // UNROLL, backward, 0)

    cols_done(dw_col, dw_colin, wc_s, wc_r)
    mine = jnp.sum(dw_colin[...].reshape(32, 128), axis=0, keepdims=True) * (1.0 / math.sqrt(49152.0))
    dw_sum[...] = jnp.broadcast_to(mine.reshape(1, 1, 128), (32, 1, 128))
    to_cols(dw_sum, dw_all, wg_s, wg_r)
    dw_all[c] = dw_sum[c]
    lax.fori_loop(128 // UNROLL, 256 // UNROLL, backward, 0)

    rz = Reduce(hg_out, hg_in, lambda half: (half_rows[half],), r, lambda pos: {"row": pos, "col": c}, hg_s, hg_r)

    def finish(pos):
        for j in range(3):
            hg_out[pos, pl.ds(j * 128, 128), :] = run[lasts_s[0, pos * 3 + j]].astype(BF16)

    finish(rz.across)
    rz.send_across()
    finish(rz.right)
    rz.send_right()
    finish(rz.left)
    rz.send_left()
    finish(r)

    cols_done(dw_sum, dw_all, wg_s, wg_r)
    dw_full[r] = dw_all[...].reshape(32, 128)
    wa = to_rows(lambda to: dw_full.at[r], dw_full, wa_s, wa_r)

    rz.relay()
    hidden_grad = jnp.concatenate([rz.total(0), rz.total(1)], axis=0).astype(BF16)
    for j in range(3):
        fg_out[pl.ds(j * 128, 128), :] = mm(weight[...], hidden_grad[j * 128:(j + 1) * 128]).T.astype(BF16)
    rz.sent()
    done(wa)
    wg_out[...] = dw_full[...].reshape(128, 128)


def local(features, weight, tiles, tile_dest, tile_src, tile_count, source_of, out_grad):
    def V(*shape, dtype=BF16):
        return pltpu.VMEM(shape, dtype)

    def D(*n):
        return pltpu.SemaphoreType.DMA(n) if n else pltpu.SemaphoreType.DMA

    I32 = jnp.int32
    scratch = [
        V(256, 128, 128), V(257, 128, 128, dtype=F32), V(4, 384, 128), V(128, 128), V(384, 128),
        V(1, 256, dtype=I32), V(1, 256, dtype=I32), V(384, dtype=I32),
        pltpu.SMEM((1, 256), I32), pltpu.SMEM((1, 256), I32),
        V(1, 256, dtype=I32), V(1, 256, dtype=I32), V(1, 128, dtype=I32), V(1, 128, dtype=I32),
        pltpu.SMEM((1, 256), I32), pltpu.SMEM((1, 256), I32), pltpu.SMEM((1, 128), I32), pltpu.SMEM((1, 128), I32),
        V(384, 384), V(384, 384), V(512, 384), V(384, 512), V(512, 384), V(384, 512),
        V(4, 96, 128), V(4, 96, 128), V(32, 16, 128), V(32, 16, 128),
        V(32, 16, 128), V(32, 16, 128), V(4, 96, 128), V(4, 96, 128),
        V(4, 96, 128), V(4, 96, 128), V(32, 16, 128), V(32, 16, 128),
        V(4, 4, 192, 128), V(4, 4, 192, 128), V(4, 4, 192, 128), V(4, 4, 192, 128),
        V(4, 4, 192, 128), V(4, 4, 192, 128), V(6, 2, 192, 128), V(6, 2, 192, 128),
        V(4, 192, 128), V(4, 192, 128), V(4, 192, 128), V(4, 192, 128),
        V(384, 128, dtype=F32), V(4, 4, 2, 2, 192, 128), V(4, 384, 128), V(6, 192, 128),
        V(4, 32, 128, dtype=F32), V(4, 32, 128, dtype=F32), V(32, 1, 128, dtype=F32), V(32, 1, 128, dtype=F32),
        V(32, 1, 128, dtype=F32), V(32, 1, 128, dtype=F32), V(4, 32, 128, dtype=F32),
        D(8), D(4), D(4),
        D(6), D(6), D(3), D(3), D(), D(), D(), D(), D(3), D(3), D(3), D(3), D(), D(),
        D(4), D(4), D(4), D(4), D(6), D(6), D(6), D(6), D(3), D(3), D(3), D(3),
        D(3), D(3), D(3), D(3), D(6), D(6), D(6), D(6), D(8), D(8),
        D(6), D(6), D(3), D(3), D(), D(), D(), D(), D(3), D(3),
    ]
    smem = pl.BlockSpec(memory_space=pltpu.SMEM)
    vmem = pl.BlockSpec(memory_space=pltpu.VMEM)
    where = pl.BlockSpec(memory_space=pl.ANY)
    return pl.pallas_call(
        kernel,
        out_shape=(
            jax.ShapeDtypeStruct((384, 128), BF16),
            jax.ShapeDtypeStruct((384, 128), BF16),
            jax.ShapeDtypeStruct((128, 128), F32),
        ),
        in_specs=[where, where, smem] + [where] * 5,
        out_specs=(vmem, vmem, vmem),
        scratch_shapes=scratch,
        compiler_params=pltpu.CompilerParams(
            collective_id=0, has_side_effects=True, vmem_limit_bytes=56 * 2**20),
    )(tile_dest, tile_src, tile_count, source_of, features, weight, out_grad, tiles[0])


def solution(mesh):
    placed = (
        P(("row", "col"), None),
        P(),
        P("row", "col", None, None),
        P("row", "col"),
        P("row", "col"),
        P("row", "col"),
        P(("row", "col")),
        P(("row", "col"), None),
    )
    return jax.shard_map(
        local,
        mesh=mesh,
        in_specs=placed,
        out_specs=(P(("row", "col"), None), P(("row", "col"), None), P()),
        check_vma=False,
    )
```

```python
import functools
import math

import jax
import jax.numpy as jnp
from jax import lax
from jax.experimental import pallas as pl
from jax.experimental.pallas import tpu as pltpu
from jax.sharding import PartitionSpec as P

MESH = pl.DeviceIdType.MESH
F32 = jnp.float32
BF16 = jnp.bfloat16
UNROLL = 64


def mm(a, b):
    return jnp.dot(a, b, preferred_element_type=F32)


def sigmoid(v):
    return 1.0 / (1.0 + jnp.exp(-v))


def iota(shape, dim):
    return lax.broadcasted_iota(jnp.int32, shape, dim)


def kernel(
    dest_h, src_h, count_s, owner_h, feat_h, weight_h, grad_h, tiles_h,
    act_out, fg_out, wg_out,
    tiles, run, fall, weight, out_grad, dest_v, src_v, owner_v,
    dest_s, src_s, prevd_v, prevs_v, lastd_v, lasts_v, prevd_s, prevs_s, lastd_s, lasts_s,
    place, place_t, regroup, regroup_t, pick, pick_t,
    id_m, id_z, id_g, id_c,
    og_m, og_c, og_g, og_z,
    ac_m, ac_z, ac_g, ac_c,
    sx_out, sy_out, sx_in, sy_in, x_out, y_out, x_in, y_in, x2_out, y2_out, x2_in, y2_in,
    dgrad, gath, hg_out, hg_in, dw, dw_in, dw_col, dw_colin, dw_sum, dw_all, dw_full,
    l_sem, t_sem, i_sem,
    f_s, f_r, idz_s, idz_r, idc_s, idc_r, ogc_s, ogc_r, ogz_s, ogz_r, acz_s, acz_r, acc_s, acc_r,
    sx_s, sx_r, sy_s, sy_r, rx_s, rx_r, ry_s, ry_r, rx2_s, rx2_r, ry2_s, ry2_r,
    ax_s, ax_r, ay_s, ay_r, gx_s, gx_r, gy_s, gy_r, as_s, as_r,
    hg_s, hg_r, wz_s, wz_r, wc_s, wc_r, wg_s, wg_r, wa_s, wa_r,
):
    r = lax.axis_index("row")
    c = lax.axis_index("col")
    x = c // 8
    y = (c // 2) % 4
    e = c % 2

    def at_chip(px, py):
        return {"row": r, "col": px * 8 + py * 2 + e}

    sibling = {"row": r, "col": x * 8 + y * 2 + (1 - e)}

    def send(src, dst, ss, rs, device):
        cp = pltpu.make_async_remote_copy(
            src_ref=src, dst_ref=dst, send_sem=ss, recv_sem=rs,
            device_id=device, device_id_type=MESH)
        cp.start()
        return cp

    def arrived(view, sem):
        pltpu.make_async_copy(view, view, sem).wait()

    def to_rows(src_of, dst, ss, rs):
        out = []
        for d in (2, 1, 3):
            to = lax.rem(r + d, 4)
            out.append(send(src_of(to), dst.at[r], ss.at[d - 1], rs.at[d - 1], {"row": to, "col": c}))
        return out

    def to_cols(src, dst, ss, rs):
        def one(d, carry):
            to = lax.rem(c + d, 32)
            send(src.at[to], dst.at[c], ss, rs, {"row": r, "col": to})
            return carry
        lax.fori_loop(1, 32, one, 0)

    def cols_done(src, dst, ss, rs):
        arrived(src.at[pl.ds(0, 31)], ss)
        arrived(dst.at[pl.ds(0, 31)], rs)

    def done(copies):
        for cp in copies:
            cp.wait()

    class Gather:
        def __init__(self, view, me, device, ss, rs):
            self.view, self.ss, self.rs = view, ss, rs
            self.right, self.left = lax.rem(me + 1, 4), lax.rem(me + 3, 4)
            self.to_right, self.to_left = device(self.right), device(self.left)
            self.copies = {}
            for n, half, device in ((0, 0, self.to_right), (2, 1, self.to_left), (1, 1, self.to_right), (3, 0, self.to_left)):
                self.go(n, view(me, half), device)

        def go(self, n, ref, device):
            self.copies[n] = send(ref, ref, self.ss.at[n], self.rs.at[n], device)

        def relay(self):
            self.copies[0].wait_recv()
            self.go(4, self.view(self.left, 0), self.to_right)
            self.copies[2].wait_recv()
            self.go(5, self.view(self.right, 1), self.to_left)

        def near(self):
            self.copies[1].wait_recv()
            self.copies[3].wait_recv()

        def far(self):
            self.copies[4].wait_recv()
            self.copies[5].wait_recv()

        def sent(self):
            for n in range(6):
                self.copies[n].wait_send()

    class Reduce:
        def __init__(self, out, into, half, me, device, ss, rs):
            self.out, self.into, self.half, self.me = out, into, half, me
            self.ss, self.rs = ss, rs
            self.right, self.left = lax.rem(me + 1, 4), lax.rem(me + 3, 4)
            self.across = lax.rem(me + 2, 4)
            self.to_right, self.to_left = device(self.right), device(self.left)
            self.copies = {}

        def go(self, n, pos, half, device):
            self.copies[n] = send(
                self.out.at[(pos,) + self.half(half)], self.into.at[n], self.ss.at[n], self.rs.at[n], device)

        def send_across(self):
            self.go(0, self.across, 0, self.to_right)
            self.go(2, self.across, 1, self.to_left)

        def send_right(self):
            self.go(1, self.right, 1, self.to_right)

        def send_left(self):
            self.go(3, self.left, 0, self.to_left)

        def relay(self):
            for n, pos, half, device in ((0, self.right, 0, self.to_right), (2, self.left, 1, self.to_left)):
                self.copies[n].wait_recv()
                at = (pos,) + self.half(half)
                self.out[at] = (self.out[at].astype(F32) + self.into[n].astype(F32)).astype(BF16)
                self.go(4 + n // 2, pos, half, device)

        def total(self, half):
            first, second = ((3, 4), (1, 5))[half]
            self.copies[first].wait_recv()
            own = self.out[(self.me,) + self.half(half)].astype(F32) + self.into[first].astype(F32)
            self.copies[second].wait_recv()
            return own + self.into[second].astype(F32)

        def sent(self):
            for n in range(6):
                self.copies[n].wait_send()

    barrier = pltpu.get_barrier_semaphore()

    def greet(d, carry):
        pl.semaphore_signal(barrier, inc=1, device_id={"row": r, "col": lax.rem(c + d, 32)}, device_id_type=MESH)
        return carry
    lax.fori_loop(1, 32, greet, 0)
    for d in range(1, 4):
        pl.semaphore_signal(barrier, inc=1, device_id={"row": lax.rem(r + d, 4), "col": c}, device_id_type=MESH)

    def load(n, src, dst):
        cp = pltpu.make_async_copy(src, dst, l_sem.at[n])
        cp.start()
        return cp

    feat_load = load(0, feat_h, fall.at[r])
    key_loads = [load(1, dest_h, dest_v), load(2, src_h, src_v), load(3, owner_h, owner_v)]
    scalar_loads = [load(4, dest_h, dest_s), load(5, src_h, src_s)]
    later_loads = [load(6, weight_h, weight), load(7, grad_h, out_grad)]
    tile_loads = [pltpu.make_async_copy(tiles_h.at[pl.ds(64 * k, 64)], tiles.at[pl.ds(64 * k, 64)], t_sem.at[k]) for k in range(4)]
    for cp in tile_loads:
        cp.start()
    feat_load.wait()
    pl.semaphore_wait(barrier, 34)

    features = to_rows(lambda to: fall.at[r], fall, f_s, f_r)
    done(key_loads)

    def wide(piece):
        return jnp.concatenate([piece] * 3, axis=1)

    source_of = owner_v[...].reshape(1, 384).astype(F32)
    owner = jnp.floor((source_of + 0.5) * (1.0 / 384.0))
    number = source_of - owner * 384.0
    owner_col = wide(jnp.broadcast_to(owner, (128, 384)).T)
    earlier = (owner_col == owner) & (iota((384, 384), 0) < iota((384, 384), 1))
    rank = jnp.sum(jnp.where(earlier, 1.0, 0.0), axis=0, keepdims=True)
    spot = owner * 3.0 + rank
    four = owner * 4.0 + rank
    four_col = jnp.broadcast_to(four, (128, 384)).T
    four_col = jnp.concatenate([four_col] * 4, axis=1)
    lanes = jnp.where(four_col == iota((384, 512), 1).astype(F32), 1.0, 0.0).astype(BF16)
    upper = jnp.floor(number * 0.5)
    parts = jnp.where(iota((16, 384), 0) == 0, upper, number - 2.0 * upper).astype(BF16)
    sent = mm(parts, lanes).astype(BF16)
    for k in range(4):
        id_m[k] = sent[:, k * 128:(k + 1) * 128]
    idz = to_rows(lambda to: id_m.at[to], id_z, idz_s, idz_r)
    id_z[r] = id_m[r]

    live = count_s[0, 0]

    def chains(key_v, prev_v, last_v, prev_s, last_s, n):
        key = key_v[...]
        col = jnp.broadcast_to(key, (128, 256)).T
        flipped = jnp.concatenate([col, col], axis=1)
        at = iota((256, 256), 0)
        before = jnp.where((flipped == key) & (at < iota((256, 256), 1)), at, -1)
        best = jnp.max(before, axis=0, keepdims=True)
        prev_v[...] = jnp.where(best < 0, 256, best)
        at = iota((256, 128), 0)
        named = jnp.where((col == iota((256, 128), 1)) & (at < live), at, -1)
        best = jnp.max(named, axis=0, keepdims=True)
        last_v[...] = jnp.where(best < 0, 256, best)
        return [pltpu.make_async_copy(prev_v, prev_s, i_sem.at[n]), pltpu.make_async_copy(last_v, last_s, i_sem.at[n + 1])]

    index_loads = chains(dest_v, prevd_v, lastd_v, prevd_s, lastd_s, 0) + chains(src_v, prevs_v, lasts_v, prevs_s, lasts_s, 2)
    for cp in index_loads:
        cp.start()

    row = iota((512, 128), 0)
    finds = jnp.where(iota((512, 128), 1) == (row >> 4) * 4 + (row & 3), 1.0, 0.0).astype(BF16)
    done(idz)
    found = lax.dot_general(finds, id_z[...].reshape(64, 128), (((1,), (1,)), ((), ())), preferred_element_type=F32)
    lane = iota((512, 64), 1) - ((iota((512, 64), 0) >> 2) & 3) * 16
    upper = jnp.sum(jnp.where(lane == 0, found, 0.0), axis=1, keepdims=True)
    lower = jnp.sum(jnp.where(lane == 1, found, 0.0), axis=1, keepdims=True)
    id_g[...] = jnp.where(iota((512, 128), 1) < 64, upper, lower).astype(BF16).reshape(32, 16, 128)
    to_cols(id_g, id_c, idc_s, idc_r)
    id_c[c] = id_g[c]

    run[256] = jnp.zeros((128, 128), F32)

    def spread(q, s):
        wanted = ((q >> 2) & 3) * 96 + (q >> 4) * 3 + (q & 3)
        return jnp.where(((q & 3) < 3) & (s == wanted), 1.0, 0.0).astype(BF16)

    regroup[...] = spread(iota((512, 384), 0), iota((512, 384), 1))
    regroup_t[...] = spread(iota((384, 512), 1), iota((384, 512), 0))
    place[...] = jnp.where(iota((384, 384), 0).astype(F32) == spot, 1.0, 0.0).astype(BF16)
    spot_col = wide(jnp.broadcast_to(spot, (128, 384)).T)
    place_t[...] = jnp.where(spot_col == iota((384, 384), 1).astype(F32), 1.0, 0.0).astype(BF16)
    done(index_loads)
    done(scalar_loads)
    done(tile_loads)
    for cp in features:
        cp.wait_recv()

    blocks = fall.reshape(12, 128, 128)

    def forward(i, carry):
        for k in range(UNROLL):
            t = i * UNROLL + k
            run[t] = run[prevd_s[0, t]] + mm(tiles[t], blocks[src_s[0, t]])
        return carry
    lax.fori_loop(0, 256 // UNROLL, forward, 0)

    steps = (("x", 2), ("y", 2), ("x", 1), ("x", 3), ("y", 1), ("y", 3), ("x", 0), ("y", 0))

    def first_rows(chip, core):
        b = (chip * 2 + core) * 3
        return run[lastd_s[0, b]], run[lastd_s[0, b + 1], pl.ds(0, 64), :]

    def last_rows(chip, core):
        b = (chip * 2 + core) * 3
        return run[lastd_s[0, b + 1], pl.ds(64, 64), :], run[lastd_s[0, b + 2]]

    sib = {}
    for axis, d in steps:
        if axis == "x":
            g = lax.rem(x + d, 4)
            for k in range(4):
                rows0, rows1 = first_rows(g * 4 + k, 1 - e)
                sx_out[g, k, pl.ds(0, 128), :] = rows0.astype(BF16)
                sx_out[g, k, pl.ds(128, 64), :] = rows1.astype(BF16)
            sib[axis, d] = send(sx_out.at[g], sx_in.at[g], sx_s.at[d], sx_r.at[d], sibling)
        else:
            g = lax.rem(y + d, 4)
            for k in range(4):
                rows0, rows1 = last_rows(k * 4 + g, 1 - e)
                sy_out[g, k, pl.ds(0, 64), :] = rows0.astype(BF16)
                sy_out[g, k, pl.ds(64, 128), :] = rows1.astype(BF16)
            sib[axis, d] = send(sy_out.at[g], sy_in.at[g], sy_s.at[d], sy_r.at[d], sibling)

    done(later_loads)
    cols_done(id_g, id_c, idc_s, idc_r)
    numbers = id_c[...].reshape(512, 128).astype(F32)
    swapped = jnp.concatenate([numbers[:, 64:128], numbers[:, 0:64]], axis=1)
    low_lane = iota((512, 128), 1) < 64
    slot_id = 2.0 * jnp.where(low_lane, numbers, swapped) + jnp.where(low_lane, swapped, numbers)
    slot_id = jnp.where((iota((512, 128), 0) & 3) < 3, slot_id, -1.0)
    pick[...] = jnp.where(wide(slot_id) == iota((512, 384), 1).astype(F32), 1.0, 0.0).astype(BF16)
    og_m[...] = mm(pick[...], out_grad[...]).astype(BF16).reshape(32, 16, 128)
    to_cols(og_m, og_c, ogc_s, ogc_r)
    og_c[c] = og_m[c]

    def pair(half):
        return (pl.ds(2 * half, 2),)

    rx = Reduce(x_out, x_in, pair, x, lambda pos: at_chip(pos, y), rx_s, rx_r)
    ry = Reduce(y_out, y_in, pair, y, lambda pos: at_chip(x, pos), ry_s, ry_r)
    for axis, d in steps:
        sib[axis, d].wait_recv()
        if axis == "x":
            g = lax.rem(x + d, 4)
            for k in range(4):
                rows0, rows1 = first_rows(g * 4 + k, e)
                x_out[g, k, pl.ds(0, 128), :] = (rows0 + sx_in[g, k, pl.ds(0, 128), :].astype(F32)).astype(BF16)
                x_out[g, k, pl.ds(128, 64), :] = (rows1 + sx_in[g, k, pl.ds(128, 64), :].astype(F32)).astype(BF16)
        else:
            g = lax.rem(y + d, 4)
            for k in range(4):
                rows0, rows1 = last_rows(k * 4 + g, e)
                y_out[g, k, pl.ds(0, 64), :] = (rows0 + sy_in[g, k, pl.ds(0, 64), :].astype(F32)).astype(BF16)
                y_out[g, k, pl.ds(64, 128), :] = (rows1 + sy_in[g, k, pl.ds(64, 128), :].astype(F32)).astype(BF16)
        ring = rx if axis == "x" else ry
        if d == 2:
            ring.send_across()
        elif d == 1:
            ring.send_right()
        elif d == 3:
            ring.send_left()

    cols_done(og_m, og_c, ogc_s, ogc_r)
    og_g[...] = mm(regroup_t[...], og_c[...].reshape(512, 128)).astype(BF16).reshape(4, 96, 128)
    ogz = to_rows(lambda to: og_g.at[to], og_z, ogz_s, ogz_r)
    og_z[r] = og_g[r]

    rx.relay()
    ry.relay()

    slot_row = slot_id.T
    slot_row = jnp.concatenate([slot_row] * 3, axis=0)
    pick_t[...] = jnp.where(slot_row == iota((384, 512), 0).astype(F32), 1.0, 0.0).astype(BF16)

    rx2, ry2 = [], []
    for half in range(2):
        x2_out[pl.ds(2 * half, 2)] = rx.total(half).astype(BF16)
    for d in (2, 1, 3):
        py = lax.rem(y + d, 4)
        rx2.append(send(x2_out.at[py], x2_in.at[y], rx2_s.at[d - 1], rx2_r.at[d - 1], at_chip(x, py)))
    for half in range(2):
        y2_out[pl.ds(2 * half, 2)] = ry.total(half).astype(BF16)
    for d in (2, 1, 3):
        px = lax.rem(x + d, 4)
        ry2.append(send(y2_out.at[px], y2_in.at[x], ry2_s.at[d - 1], ry2_r.at[d - 1], at_chip(px, y)))

    done(ogz)
    dgrad[...] = mm(place_t[...], og_z[...].reshape(384, 128))
    rx.sent()
    ry.sent()
    for step in steps:
        sib[step].wait_send()
    for cp in features:
        cp.wait_send()

    done(rx2)
    top = x2_out[y].astype(F32)
    for d in range(1, 4):
        top += x2_in[lax.rem(y + d, 4)].astype(F32)
    done(ry2)
    low = y2_out[x].astype(F32)
    for d in range(1, 4):
        low += y2_in[lax.rem(x + d, 4)].astype(F32)
    sums = jnp.concatenate([top, low], axis=0)
    sums_high = sums.astype(BF16)
    sums_low = (sums - sums_high.astype(F32)).astype(BF16)
    pre = (mm(sums_high, weight[...]) + mm(sums_low, weight[...])).astype(BF16).astype(F32)
    sg = sigmoid(pre)
    grad = (dgrad[...] * (sg * (1.0 + pre * (1.0 - sg)))).astype(BF16).astype(F32)
    turned = [grad[j * 128:(j + 1) * 128].T.astype(BF16) for j in range(3)]
    gath[x, y, e, 0, pl.ds(0, 128), :] = turned[0]
    gath[x, y, e, 0, pl.ds(128, 64), :] = turned[1][0:64]
    gath[x, y, e, 1, pl.ds(0, 64), :] = turned[1][64:128]
    gath[x, y, e, 1, pl.ds(64, 128), :] = turned[2]

    ax, ay = [], []
    for d in (2, 1, 3):
        part = gath.at[x, y, e, 0]
        ax.append(send(part, part, ax_s.at[d - 1], ax_r.at[d - 1], at_chip(lax.rem(x + d, 4), y)))
        part = gath.at[x, y, e, 1]
        ay.append(send(part, part, ay_s.at[d - 1], ay_r.at[d - 1], at_chip(x, lax.rem(y + d, 4))))

    ac_m[...] = mm(place[...], (pre * sg).astype(BF16)).astype(BF16).reshape(4, 96, 128)
    acz = to_rows(lambda to: ac_m.at[to], ac_z, acz_s, acz_r)
    ac_z[r] = ac_m[r]
    term = jnp.zeros((128, 128), F32)
    for j in range(3):
        rows = slice(j * 128, (j + 1) * 128)
        term += mm(turned[j], sums_high[rows]) + mm(turned[j], sums_low[rows])
    dw[...] = term.T.reshape(4, 32, 128)
    wz = to_rows(lambda to: dw.at[to], dw_in, wz_s, wz_r)

    done(ax)
    by_y = Gather(lambda pos, half: gath.at[pl.ds(2 * half, 2), pos, e, 0], y, lambda pos: at_chip(x, pos), gy_s, gy_r)
    done(ay)
    by_x = Gather(lambda pos, half: gath.at[pos, pl.ds(2 * half, 2), e, 1], x, lambda pos: at_chip(pos, y), gx_s, gx_r)
    asib = []

    def share(n, part):
        asib.append(send(part, part, as_s.at[n], as_r.at[n], sibling))

    share(0, gath.at[:, y, e, 0])
    share(1, gath.at[x, :, e, 1])

    done(acz)
    ac_g[...] = mm(regroup[...], ac_z[...].reshape(384, 128)).astype(BF16).reshape(32, 16, 128)
    to_cols(ac_g, ac_c, acc_s, acc_r)
    ac_c[c] = ac_g[c]

    by_y.relay()
    by_x.relay()
    by_y.near()
    share(2, gath.at[:, by_y.left, e, 0])
    share(3, gath.at[:, by_y.right, e, 0])
    by_x.near()
    share(4, gath.at[by_x.left, :, e, 1])
    share(5, gath.at[by_x.right, :, e, 1])

    done(wz)
    total = dw[r]
    for d in range(1, 4):
        total += dw_in[lax.rem(r + d, 4)]
    dw_col[...] = total.reshape(32, 1, 128)
    to_cols(dw_col, dw_colin, wc_s, wc_r)
    dw_colin[c] = dw_col[c]

    for half in range(2):
        by_y.copies[4 + half].wait_recv()
        share(6 + half, by_y.view(lax.rem(y + 2, 4), half))
        by_x.copies[4 + half].wait_recv()
        share(8 + half, by_x.view(lax.rem(x + 2, 4), half))

    cols_done(ac_g, ac_c, acc_s, acc_r)
    act_out[...] = mm(pick_t[...], ac_c[...].reshape(512, 128)).astype(BF16)
    by_y.sent()
    by_x.sent()
    done(asib)

    grads = gath.reshape(96, 128, 128)

    def backward(i, carry):
        for k in range(UNROLL):
            t = i * UNROLL + k
            run[t] = run[prevs_s[0, t]] + mm(grads[dest_s[0, t]], tiles[t])
        return carry
    lax.fori_loop(0, 128 // UNROLL, backward, 0)

    cols_done(dw_col, dw_colin, wc_s, wc_r)
    mine = jnp.sum(dw_colin[...].reshape(32, 128), axis=0, keepdims=True) * (1.0 / math.sqrt(49152.0))
    dw_sum[...] = jnp.broadcast_to(mine.reshape(1, 1, 128), (32, 1, 128))
    to_cols(dw_sum, dw_all, wg_s, wg_r)
    dw_all[c] = dw_sum[c]
    lax.fori_loop(128 // UNROLL, 256 // UNROLL, backward, 0)

    def finish(pos):
        for j in range(3):
            hg_out[pos, pl.ds(j * 128, 128), :] = run[lasts_s[0, pos * 3 + j]].astype(BF16)

    hgc = []
    for d in (2, 1, 3):
        to = lax.rem(r + d, 4)
        finish(to)
        hgc.append(send(hg_out.at[to], hg_in.at[d - 1], hg_s.at[d - 1], hg_r.at[d - 1], {"row": to, "col": c}))
    finish(r)

    cols_done(dw_sum, dw_all, wg_s, wg_r)
    dw_full[r] = dw_all[...].reshape(32, 128)
    wa = to_rows(lambda to: dw_full.at[r], dw_full, wa_s, wa_r)

    total = hg_out[r].astype(F32)
    for n, d in ((1, 1), (2, 3), (0, 2)):
        hgc[n].wait_recv()
        total += hg_in[d - 1].astype(F32)
    hidden_grad = total.astype(BF16)
    for j in range(3):
        fg_out[pl.ds(j * 128, 128), :] = mm(weight[...], hidden_grad[j * 128:(j + 1) * 128]).T.astype(BF16)
    for cp in hgc:
        cp.wait_send()
    done(wa)
    wg_out[...] = dw_full[...].reshape(128, 128)


def local(features, weight, tiles, tile_dest, tile_src, tile_count, source_of, out_grad):
    def V(*shape, dtype=BF16):
        return pltpu.VMEM(shape, dtype)

    def D(*n):
        return pltpu.SemaphoreType.DMA(n) if n else pltpu.SemaphoreType.DMA

    I32 = jnp.int32
    scratch = [
        V(256, 128, 128), V(257, 128, 128, dtype=F32), V(4, 384, 128), V(128, 128), V(384, 128),
        V(1, 256, dtype=I32), V(1, 256, dtype=I32), V(384, dtype=I32),
        pltpu.SMEM((1, 256), I32), pltpu.SMEM((1, 256), I32),
        V(1, 256, dtype=I32), V(1, 256, dtype=I32), V(1, 128, dtype=I32), V(1, 128, dtype=I32),
        pltpu.SMEM((1, 256), I32), pltpu.SMEM((1, 256), I32), pltpu.SMEM((1, 128), I32), pltpu.SMEM((1, 128), I32),
        V(384, 384), V(384, 384), V(512, 384), V(384, 512), V(512, 384), V(384, 512),
        V(4, 16, 128), V(4, 16, 128), V(32, 16, 128), V(32, 16, 128),
        V(32, 16, 128), V(32, 16, 128), V(4, 96, 128), V(4, 96, 128),
        V(4, 96, 128), V(4, 96, 128), V(32, 16, 128), V(32, 16, 128),
        V(4, 4, 192, 128), V(4, 4, 192, 128), V(4, 4, 192, 128), V(4, 4, 192, 128),
        V(4, 4, 192, 128), V(4, 4, 192, 128), V(6, 2, 192, 128), V(6, 2, 192, 128),
        V(4, 192, 128), V(4, 192, 128), V(4, 192, 128), V(4, 192, 128),
        V(384, 128, dtype=F32), V(4, 4, 2, 2, 192, 128), V(4, 384, 128), V(3, 384, 128),
        V(4, 32, 128, dtype=F32), V(4, 32, 128, dtype=F32), V(32, 1, 128, dtype=F32), V(32, 1, 128, dtype=F32),
        V(32, 1, 128, dtype=F32), V(32, 1, 128, dtype=F32), V(4, 32, 128, dtype=F32),
        D(8), D(4), D(4),
        D(6), D(6), D(3), D(3), D(), D(), D(), D(), D(3), D(3), D(3), D(3), D(), D(),
        D(4), D(4), D(4), D(4), D(6), D(6), D(6), D(6), D(3), D(3), D(3), D(3),
        D(3), D(3), D(3), D(3), D(6), D(6), D(6), D(6), D(10), D(10),
        D(6), D(6), D(3), D(3), D(), D(), D(), D(), D(3), D(3),
    ]
    smem = pl.BlockSpec(memory_space=pltpu.SMEM)
    vmem = pl.BlockSpec(memory_space=pltpu.VMEM)
    where = pl.BlockSpec(memory_space=pl.ANY)
    return pl.pallas_call(
        kernel,
        out_shape=(
            pltpu.VMEM((384, 128), BF16),
            pltpu.VMEM((384, 128), BF16),
            pltpu.VMEM((128, 128), F32),
        ),
        in_specs=[where, where, smem] + [where] * 5,
        out_specs=(vmem, vmem, vmem),
        scratch_shapes=scratch,
        compiler_params=pltpu.CompilerParams(
            collective_id=0, has_side_effects=True, vmem_limit_bytes=56 * 2**20),
    )(tile_dest, tile_src, tile_count, source_of, features, weight, out_grad, tiles[0])


def solution(mesh):
    placed = (
        P(("row", "col"), None),
        P(),
        P("row", "col", None, None),
        P("row", "col"),
        P("row", "col"),
        P("row", "col"),
        P(("row", "col")),
        P(("row", "col"), None),
    )
    return jax.shard_map(
        local,
        mesh=mesh,
        in_specs=placed,
        out_specs=(P(("row", "col"), None), P(("row", "col"), None), P()),
        check_vma=False,
    )
```

```python
import functools
import math

import jax
import jax.numpy as jnp
from jax import lax
from jax.experimental import pallas as pl
from jax.experimental.pallas import tpu as pltpu
from jax.sharding import PartitionSpec as P

MESH = pl.DeviceIdType.MESH
F32 = jnp.float32
BF16 = jnp.bfloat16
UNROLL = 64


def mm(a, b):
    return jnp.dot(a, b, preferred_element_type=F32)


def sigmoid(v):
    return 1.0 / (1.0 + jnp.exp(-v))


def iota(shape, dim):
    return lax.broadcasted_iota(jnp.int32, shape, dim)


def kernel(
    dest_h, src_h, count_s, owner_h, feat_h, weight_h, grad_h, tiles_h,
    act_out, fg_out, wg_out,
    tiles, run, fall, weight, out_grad, dest_v, src_v, owner_v,
    dest_s, src_s, prevd_v, prevs_v, lastd_v, lasts_v, prevd_s, prevs_s, lastd_s, lasts_s,
    place, place_t, regroup, regroup_t, pick, pick_t,
    id_m, id_z, id_g, id_c,
    og_m, og_c, og_g, og_z,
    ac_m, ac_z, ac_g, ac_c,
    sx_out, sy_out, sx_in, sy_in, x_out, y_out, x_in, y_in, x2_out, y2_out, x2_in, y2_in,
    dgrad, gath, hg_out, hg_in, dw, dw_in, dw_all, dw_full, spare,
    l_sem, t_sem, i_sem,
    f_s, f_r, idz_s, idz_r, idc_s, idc_r, ogc_s, ogc_r, ogz_s, ogz_r, acz_s, acz_r, acc_s, acc_r,
    sx_s, sx_r, sy_s, sy_r, rx_s, rx_r, ry_s, ry_r, rx2_s, rx2_r, ry2_s, ry2_r,
    ax_s, ax_r, ay_s, ay_r, gx_s, gx_r, gy_s, gy_r, as_s, as_r,
    hg_s, hg_r, wz_s, wz_r, wg_s, wg_r, wa_s, wa_r,
):
    r = lax.axis_index("row")
    c = lax.axis_index("col")
    x = c // 8
    y = (c // 2) % 4
    e = c % 2

    def at_chip(px, py):
        return {"row": r, "col": px * 8 + py * 2 + e}

    sibling = {"row": r, "col": x * 8 + y * 2 + (1 - e)}

    def send(src, dst, ss, rs, device):
        cp = pltpu.make_async_remote_copy(
            src_ref=src, dst_ref=dst, send_sem=ss, recv_sem=rs,
            device_id=device, device_id_type=MESH)
        cp.start()
        return cp

    def arrived(view, sem):
        pltpu.make_async_copy(view, view, sem).wait()

    def to_rows(src_of, dst, ss, rs):
        out = []
        for d in (2, 1, 3):
            to = lax.rem(r + d, 4)
            out.append(send(src_of(to), dst.at[r], ss.at[d - 1], rs.at[d - 1], {"row": to, "col": c}))
        return out

    def to_cols(src, dst, ss, rs):
        def one(d, carry):
            to = lax.rem(c + d, 32)
            send(src.at[to], dst.at[c], ss, rs, {"row": r, "col": to})
            return carry
        lax.fori_loop(1, 32, one, 0)

    def cols_done(src, dst, ss, rs):
        arrived(src.at[pl.ds(0, 31)], ss)
        arrived(dst.at[pl.ds(0, 31)], rs)

    def done(copies):
        for cp in copies:
            cp.wait()

    class Gather:
        def __init__(self, view, me, device, ss, rs):
            self.view, self.ss, self.rs = view, ss, rs
            self.right, self.left = lax.rem(me + 1, 4), lax.rem(me + 3, 4)
            self.to_right, self.to_left = device(self.right), device(self.left)
            self.copies = {}
            for n, half, device in ((0, 0, self.to_right), (2, 1, self.to_left), (1, 1, self.to_right), (3, 0, self.to_left)):
                self.go(n, view(me, half), device)

        def go(self, n, ref, device):
            self.copies[n] = send(ref, ref, self.ss.at[n], self.rs.at[n], device)

        def relay(self):
            self.copies[0].wait_recv()
            self.go(4, self.view(self.left, 0), self.to_right)
            self.copies[2].wait_recv()
            self.go(5, self.view(self.right, 1), self.to_left)

        def near(self):
            self.copies[1].wait_recv()
            self.copies[3].wait_recv()

        def far(self):
            self.copies[4].wait_recv()
            self.copies[5].wait_recv()

        def sent(self):
            for n in range(6):
                self.copies[n].wait_send()

    class Reduce:
        def __init__(self, out, into, half, me, device, ss, rs):
            self.out, self.into, self.half, self.me = out, into, half, me
            self.ss, self.rs = ss, rs
            self.right, self.left = lax.rem(me + 1, 4), lax.rem(me + 3, 4)
            self.across = lax.rem(me + 2, 4)
            self.to_right, self.to_left = device(self.right), device(self.left)
            self.copies = {}

        def go(self, n, pos, half, device):
            self.copies[n] = send(
                self.out.at[(pos,) + self.half(half)], self.into.at[n], self.ss.at[n], self.rs.at[n], device)

        def send_across(self):
            self.go(0, self.across, 0, self.to_right)
            self.go(2, self.across, 1, self.to_left)

        def send_right(self):
            self.go(1, self.right, 1, self.to_right)

        def send_left(self):
            self.go(3, self.left, 0, self.to_left)

        def relay(self):
            for n, pos, half, device in ((0, self.right, 0, self.to_right), (2, self.left, 1, self.to_left)):
                self.copies[n].wait_recv()
                at = (pos,) + self.half(half)
                self.out[at] = (self.out[at].astype(F32) + self.into[n].astype(F32)).astype(BF16)
                self.go(4 + n // 2, pos, half, device)

        def total(self, half):
            first, second = ((3, 4), (1, 5))[half]
            self.copies[first].wait_recv()
            own = self.out[(self.me,) + self.half(half)].astype(F32) + self.into[first].astype(F32)
            self.copies[second].wait_recv()
            return own + self.into[second].astype(F32)

        def sent(self):
            for n in range(6):
                self.copies[n].wait_send()

    barrier = pltpu.get_barrier_semaphore()

    def greet(d, carry):
        pl.semaphore_signal(barrier, inc=1, device_id={"row": r, "col": lax.rem(c + d, 32)}, device_id_type=MESH)
        return carry
    lax.fori_loop(1, 32, greet, 0)
    for d in range(1, 4):
        pl.semaphore_signal(barrier, inc=1, device_id={"row": lax.rem(r + d, 4), "col": c}, device_id_type=MESH)

    def load(n, src, dst):
        cp = pltpu.make_async_copy(src, dst, l_sem.at[n])
        cp.start()
        return cp

    feat_load = load(0, feat_h, fall.at[r])
    key_loads = [load(1, dest_h, dest_v), load(2, src_h, src_v), load(3, owner_h, owner_v)]
    scalar_loads = [load(4, dest_h, dest_s), load(5, src_h, src_s)]
    later_loads = [load(6, weight_h, weight), load(7, grad_h, out_grad)]
    tile_loads = [pltpu.make_async_copy(tiles_h.at[pl.ds(64 * k, 64)], tiles.at[pl.ds(64 * k, 64)], t_sem.at[k]) for k in range(4)]
    for cp in tile_loads:
        cp.start()
    feat_load.wait()
    done(key_loads)

    def wide(piece):
        return jnp.concatenate([piece] * 3, axis=1)

    source_of = owner_v[...].reshape(1, 384).astype(F32)
    owner = jnp.floor((source_of + 0.5) * (1.0 / 384.0))
    number = source_of - owner * 384.0
    owner_col = wide(jnp.broadcast_to(owner, (128, 384)).T)
    earlier = (owner_col == owner) & (iota((384, 384), 0) < iota((384, 384), 1))
    rank = jnp.sum(jnp.where(earlier, 1.0, 0.0), axis=0, keepdims=True)
    spot = owner * 3.0 + rank
    four = owner * 4.0 + rank
    four_col = jnp.broadcast_to(four, (128, 384)).T
    four_col = jnp.concatenate([four_col] * 4, axis=1)
    lanes = jnp.where(four_col == iota((384, 512), 1).astype(F32), 1.0, 0.0).astype(BF16)
    upper = jnp.floor(number * 0.5)
    parts = jnp.where(iota((16, 384), 0) == 0, upper, number - 2.0 * upper).astype(BF16)
    sent = mm(parts, lanes).astype(BF16)
    for k in range(4):
        id_m[k] = sent[:, k * 128:(k + 1) * 128]
    pl.semaphore_wait(barrier, 34)
    idz = to_rows(lambda to: id_m.at[to], id_z, idz_s, idz_r)
    id_z[r] = id_m[r]

    features = to_rows(lambda to: fall.at[r], fall, f_s, f_r)


    live = count_s[0, 0]

    def chains(key_v, prev_v, last_v, prev_s, last_s, n):
        key = key_v[...]
        col = jnp.broadcast_to(key, (128, 256)).T
        flipped = jnp.concatenate([col, col], axis=1)
        at = iota((256, 256), 0)
        before = jnp.where((flipped == key) & (at < iota((256, 256), 1)), at, -1)
        best = jnp.max(before, axis=0, keepdims=True)
        prev_v[...] = jnp.where(best < 0, 256, best)
        at = iota((256, 128), 0)
        named = jnp.where((col == iota((256, 128), 1)) & (at < live), at, -1)
        best = jnp.max(named, axis=0, keepdims=True)
        last_v[...] = jnp.where(best < 0, 256, best)
        return [pltpu.make_async_copy(prev_v, prev_s, i_sem.at[n]), pltpu.make_async_copy(last_v, last_s, i_sem.at[n + 1])]

    index_loads = chains(dest_v, prevd_v, lastd_v, prevd_s, lastd_s, 0) + chains(src_v, prevs_v, lasts_v, prevs_s, lasts_s, 2)
    for cp in index_loads:
        cp.start()

    row = iota((512, 128), 0)
    finds = jnp.where(iota((512, 128), 1) == (row >> 4) * 4 + (row & 3), 1.0, 0.0).astype(BF16)
    done(idz)
    found = lax.dot_general(finds, id_z[...].reshape(64, 128), (((1,), (1,)), ((), ())), preferred_element_type=F32)
    lane = iota((512, 64), 1) - ((iota((512, 64), 0) >> 2) & 3) * 16
    upper = jnp.sum(jnp.where(lane == 0, found, 0.0), axis=1, keepdims=True)
    lower = jnp.sum(jnp.where(lane == 1, found, 0.0), axis=1, keepdims=True)
    id_g[...] = jnp.where(iota((512, 128), 1) < 64, upper, lower).astype(BF16).reshape(32, 16, 128)
    to_cols(id_g, id_c, idc_s, idc_r)
    id_c[c] = id_g[c]

    run[256] = jnp.zeros((128, 128), F32)

    def spread(q, s):
        wanted = ((q >> 2) & 3) * 96 + (q >> 4) * 3 + (q & 3)
        return jnp.where(((q & 3) < 3) & (s == wanted), 1.0, 0.0).astype(BF16)

    regroup[...] = spread(iota((512, 384), 0), iota((512, 384), 1))
    row = iota((512, 96), 0)
    at_spare = ((row & 3) == 3) & (iota((512, 96), 1) == ((row >> 2) & 3) * 32 + (row >> 4))
    spare[...] = jnp.where(at_spare, 1.0, 0.0).astype(BF16)
    regroup_t[...] = spread(iota((384, 512), 1), iota((384, 512), 0))
    place[...] = jnp.where(iota((384, 384), 0).astype(F32) == spot, 1.0, 0.0).astype(BF16)
    spot_col = wide(jnp.broadcast_to(spot, (128, 384)).T)
    place_t[...] = jnp.where(spot_col == iota((384, 384), 1).astype(F32), 1.0, 0.0).astype(BF16)
    done(index_loads)
    done(scalar_loads)
    done(tile_loads)
    for cp in features:
        cp.wait_recv()

    blocks = fall.reshape(12, 128, 128)

    def forward(i, carry):
        for k in range(UNROLL):
            t = i * UNROLL + k
            run[t] = run[prevd_s[0, t]] + mm(tiles[t], blocks[src_s[0, t]])
        return carry
    lax.fori_loop(0, 256 // UNROLL, forward, 0)

    steps = (("x", 2), ("y", 2), ("x", 1), ("x", 3), ("y", 1), ("y", 3), ("x", 0), ("y", 0))

    def first_rows(chip, core):
        b = (chip * 2 + core) * 3
        return run[lastd_s[0, b]], run[lastd_s[0, b + 1], pl.ds(0, 64), :]

    def last_rows(chip, core):
        b = (chip * 2 + core) * 3
        return run[lastd_s[0, b + 1], pl.ds(64, 64), :], run[lastd_s[0, b + 2]]

    sib = {}
    for axis, d in steps:
        if axis == "x":
            g = lax.rem(x + d, 4)
            for k in range(4):
                rows0, rows1 = first_rows(g * 4 + k, 1 - e)
                sx_out[g, k, pl.ds(0, 128), :] = rows0.astype(BF16)
                sx_out[g, k, pl.ds(128, 64), :] = rows1.astype(BF16)
            sib[axis, d] = send(sx_out.at[g], sx_in.at[g], sx_s.at[d], sx_r.at[d], sibling)
        else:
            g = lax.rem(y + d, 4)
            for k in range(4):
                rows0, rows1 = last_rows(k * 4 + g, 1 - e)
                sy_out[g, k, pl.ds(0, 64), :] = rows0.astype(BF16)
                sy_out[g, k, pl.ds(64, 128), :] = rows1.astype(BF16)
            sib[axis, d] = send(sy_out.at[g], sy_in.at[g], sy_s.at[d], sy_r.at[d], sibling)

    done(later_loads)
    cols_done(id_g, id_c, idc_s, idc_r)
    numbers = id_c[...].reshape(512, 128).astype(F32)
    swapped = jnp.concatenate([numbers[:, 64:128], numbers[:, 0:64]], axis=1)
    low_lane = iota((512, 128), 1) < 64
    slot_id = 2.0 * jnp.where(low_lane, numbers, swapped) + jnp.where(low_lane, swapped, numbers)
    slot_id = jnp.where((iota((512, 128), 0) & 3) < 3, slot_id, -1.0)
    pick[...] = jnp.where(wide(slot_id) == iota((512, 384), 1).astype(F32), 1.0, 0.0).astype(BF16)
    og_m[...] = mm(pick[...], out_grad[...]).astype(BF16).reshape(32, 16, 128)
    to_cols(og_m, og_c, ogc_s, ogc_r)
    og_c[c] = og_m[c]

    def pair(half):
        return (pl.ds(2 * half, 2),)

    rx = Reduce(x_out, x_in, pair, x, lambda pos: at_chip(pos, y), rx_s, rx_r)
    ry = Reduce(y_out, y_in, pair, y, lambda pos: at_chip(x, pos), ry_s, ry_r)
    for axis, d in steps:
        sib[axis, d].wait_recv()
        if axis == "x":
            g = lax.rem(x + d, 4)
            for k in range(4):
                rows0, rows1 = first_rows(g * 4 + k, e)
                x_out[g, k, pl.ds(0, 128), :] = (rows0 + sx_in[g, k, pl.ds(0, 128), :].astype(F32)).astype(BF16)
                x_out[g, k, pl.ds(128, 64), :] = (rows1 + sx_in[g, k, pl.ds(128, 64), :].astype(F32)).astype(BF16)
        else:
            g = lax.rem(y + d, 4)
            for k in range(4):
                rows0, rows1 = last_rows(k * 4 + g, e)
                y_out[g, k, pl.ds(0, 64), :] = (rows0 + sy_in[g, k, pl.ds(0, 64), :].astype(F32)).astype(BF16)
                y_out[g, k, pl.ds(64, 128), :] = (rows1 + sy_in[g, k, pl.ds(64, 128), :].astype(F32)).astype(BF16)
        ring = rx if axis == "x" else ry
        if d == 2:
            ring.send_across()
        elif d == 1:
            ring.send_right()
        elif d == 3:
            ring.send_left()

    cols_done(og_m, og_c, ogc_s, ogc_r)
    og_g[...] = mm(regroup_t[...], og_c[...].reshape(512, 128)).astype(BF16).reshape(4, 96, 128)
    ogz = to_rows(lambda to: og_g.at[to], og_z, ogz_s, ogz_r)
    og_z[r] = og_g[r]

    rx.relay()
    ry.relay()

    slot_row = slot_id.T
    slot_row = jnp.concatenate([slot_row] * 3, axis=0)
    pick_t[...] = jnp.where(slot_row == iota((384, 512), 0).astype(F32), 1.0, 0.0).astype(BF16)

    rx2, ry2 = [], []
    for half in range(2):
        x2_out[pl.ds(2 * half, 2)] = rx.total(half).astype(BF16)
    for d in (2, 1, 3):
        py = lax.rem(y + d, 4)
        rx2.append(send(x2_out.at[py], x2_in.at[y], rx2_s.at[d - 1], rx2_r.at[d - 1], at_chip(x, py)))
    for half in range(2):
        y2_out[pl.ds(2 * half, 2)] = ry.total(half).astype(BF16)
    for d in (2, 1, 3):
        px = lax.rem(x + d, 4)
        ry2.append(send(y2_out.at[px], y2_in.at[x], ry2_s.at[d - 1], ry2_r.at[d - 1], at_chip(px, y)))

    done(ogz)
    dgrad[...] = mm(place_t[...], og_z[...].reshape(384, 128))
    for cp in features:
        cp.wait_send()

    done(rx2)
    top = x2_out[y].astype(F32)
    for d in range(1, 4):
        top += x2_in[lax.rem(y + d, 4)].astype(F32)
    done(ry2)
    low = y2_out[x].astype(F32)
    for d in range(1, 4):
        low += y2_in[lax.rem(x + d, 4)].astype(F32)
    sums = jnp.concatenate([top, low], axis=0)
    sums_high = sums.astype(BF16)
    sums_low = (sums - sums_high.astype(F32)).astype(BF16)
    pre = (mm(sums_high, weight[...]) + mm(sums_low, weight[...])).astype(BF16).astype(F32)
    sg = sigmoid(pre)
    grad = (dgrad[...] * (sg * (1.0 + pre * (1.0 - sg)))).astype(BF16).astype(F32)
    turned = [grad[j * 128:(j + 1) * 128].T.astype(BF16) for j in range(3)]
    gath[x, y, e, 0, pl.ds(0, 128), :] = turned[0]
    gath[x, y, e, 0, pl.ds(128, 64), :] = turned[1][0:64]
    gath[x, y, e, 1, pl.ds(0, 64), :] = turned[1][64:128]
    gath[x, y, e, 1, pl.ds(64, 128), :] = turned[2]

    ax, ay = [], []
    for d in (2, 1, 3):
        part = gath.at[x, y, e, 0]
        ax.append(send(part, part, ax_s.at[d - 1], ax_r.at[d - 1], at_chip(lax.rem(x + d, 4), y)))
        part = gath.at[x, y, e, 1]
        ay.append(send(part, part, ay_s.at[d - 1], ay_r.at[d - 1], at_chip(x, lax.rem(y + d, 4))))

    ac_m[...] = mm(place[...], (pre * sg).astype(BF16)).astype(BF16).reshape(4, 96, 128)
    acz = to_rows(lambda to: ac_m.at[to], ac_z, acz_s, acz_r)
    ac_z[r] = ac_m[r]
    term = jnp.zeros((128, 128), F32)
    for j in range(3):
        rows = slice(j * 128, (j + 1) * 128)
        term += mm(turned[j], sums_high[rows]) + mm(turned[j], sums_low[rows])
    dw[...] = term.T.reshape(4, 32, 128)
    wz = to_rows(lambda to: dw.at[to], dw_in, wz_s, wz_r)

    done(ax)
    by_y = Gather(lambda pos, half: gath.at[pl.ds(2 * half, 2), pos, e, 0], y, lambda pos: at_chip(x, pos), gy_s, gy_r)
    done(ay)
    by_x = Gather(lambda pos, half: gath.at[pos, pl.ds(2 * half, 2), e, 1], x, lambda pos: at_chip(pos, y), gx_s, gx_r)
    asib = []

    def share(n, part):
        asib.append(send(part, part, as_s.at[n], as_r.at[n], sibling))

    share(0, gath.at[:, y, e, 0])
    share(1, gath.at[x, :, e, 1])

    done(acz)
    done(wz)
    total = dw[r]
    for d in range(1, 4):
        total += dw_in[lax.rem(r + d, 4)]
    high = total.astype(BF16)
    rest = total - high.astype(F32)
    middle = rest.astype(BF16)
    low = (rest - middle.astype(F32)).astype(BF16)
    ac_g[...] = (mm(regroup[...], ac_z[...].reshape(384, 128)) + mm(spare[...], jnp.concatenate([high, middle, low], axis=0))
                 ).astype(BF16).reshape(32, 16, 128)
    to_cols(ac_g, ac_c, acc_s, acc_r)
    ac_c[c] = ac_g[c]

    by_y.relay()
    by_x.relay()
    by_y.near()
    share(2, gath.at[:, by_y.left, e, 0])
    share(3, gath.at[:, by_y.right, e, 0])
    by_x.near()
    share(4, gath.at[by_x.left, :, e, 1])
    share(5, gath.at[by_x.right, :, e, 1])

    for half in range(2):
        by_y.copies[4 + half].wait_recv()
        share(6 + half, by_y.view(lax.rem(y + 2, 4), half))
        by_x.copies[4 + half].wait_recv()
        share(8 + half, by_x.view(lax.rem(x + 2, 4), half))

    cols_done(ac_g, ac_c, acc_s, acc_r)
    came = ac_c[...].reshape(512, 128)
    act_out[...] = mm(pick_t[...], came).astype(BF16)
    ones = jnp.where((iota((16, 512), 1) & 3) == 3, 1.0, 0.0).astype(BF16)
    mine = mm(ones, came)[0:1] * (1.0 / math.sqrt(49152.0))
    dw_all[x, y, e] = mine
    w_copies = [send(dw_all.at[x, y, e], dw_all.at[x, y, e], wg_s.at[0], wg_r.at[0], sibling)]
    for cp in asib:
        cp.wait_recv()

    grads = gath.reshape(96, 128, 128)

    def backward(i, carry):
        for k in range(UNROLL):
            t = i * UNROLL + k
            run[t] = run[prevs_s[0, t]] + mm(grads[dest_s[0, t]], tiles[t])
        return carry
    lax.fori_loop(0, 128 // UNROLL, backward, 0)

    w_copies[0].wait_recv()
    for d in (2, 1, 3):
        part = dw_all.at[x, y]
        w_copies.append(send(part, part, wg_s.at[d], wg_r.at[d], at_chip(lax.rem(x + d, 4), y)))
    lax.fori_loop(128 // UNROLL, 256 // UNROLL, backward, 0)

    def finish(pos):
        for j in range(3):
            hg_out[pos, pl.ds(j * 128, 128), :] = run[lasts_s[0, pos * 3 + j]].astype(BF16)

    for cp in w_copies[1:]:
        cp.wait_recv()
    for d in (2, 1, 3):
        part = dw_all.at[:, y]
        w_copies.append(send(part, part, wg_s.at[3 + d], wg_r.at[3 + d], at_chip(x, lax.rem(y + d, 4))))

    hgc = []
    for d in (2, 1, 3):
        to = lax.rem(r + d, 4)
        finish(to)
        hgc.append(send(hg_out.at[to], hg_in.at[d - 1], hg_s.at[d - 1], hg_r.at[d - 1], {"row": to, "col": c}))
    finish(r)

    for cp in w_copies[4:]:
        cp.wait_recv()
    dw_full[r] = dw_all[...].reshape(32, 128)
    wa = to_rows(lambda to: dw_full.at[r], dw_full, wa_s, wa_r)

    by_y.sent()
    by_x.sent()
    rx.sent()
    ry.sent()
    for cp in asib + list(sib.values()):
        cp.wait_send()
    total = hg_out[r].astype(F32)
    for n, d in ((1, 1), (2, 3), (0, 2)):
        hgc[n].wait_recv()
        total += hg_in[d - 1].astype(F32)
    hidden_grad = total.astype(BF16)
    for j in range(3):
        fg_out[pl.ds(j * 128, 128), :] = mm(weight[...], hidden_grad[j * 128:(j + 1) * 128]).T.astype(BF16)
    for cp in hgc + w_copies:
        cp.wait_send()
    done(wa)
    wg_out[...] = dw_full[...].reshape(128, 128)


def local(features, weight, tiles, tile_dest, tile_src, tile_count, source_of, out_grad):
    def V(*shape, dtype=BF16):
        return pltpu.VMEM(shape, dtype)

    def D(*n):
        return pltpu.SemaphoreType.DMA(n) if n else pltpu.SemaphoreType.DMA

    I32 = jnp.int32
    scratch = [
        V(256, 128, 128), V(257, 128, 128, dtype=F32), V(4, 384, 128), V(128, 128), V(384, 128),
        V(1, 256, dtype=I32), V(1, 256, dtype=I32), V(384, dtype=I32),
        pltpu.SMEM((1, 256), I32), pltpu.SMEM((1, 256), I32),
        V(1, 256, dtype=I32), V(1, 256, dtype=I32), V(1, 128, dtype=I32), V(1, 128, dtype=I32),
        pltpu.SMEM((1, 256), I32), pltpu.SMEM((1, 256), I32), pltpu.SMEM((1, 128), I32), pltpu.SMEM((1, 128), I32),
        V(384, 384), V(384, 384), V(512, 384), V(384, 512), V(512, 384), V(384, 512),
        V(4, 16, 128), V(4, 16, 128), V(32, 16, 128), V(32, 16, 128),
        V(32, 16, 128), V(32, 16, 128), V(4, 96, 128), V(4, 96, 128),
        V(4, 96, 128), V(4, 96, 128), V(32, 16, 128), V(32, 16, 128),
        V(4, 4, 192, 128), V(4, 4, 192, 128), V(4, 4, 192, 128), V(4, 4, 192, 128),
        V(4, 4, 192, 128), V(4, 4, 192, 128), V(6, 2, 192, 128), V(6, 2, 192, 128),
        V(4, 192, 128), V(4, 192, 128), V(4, 192, 128), V(4, 192, 128),
        V(384, 128, dtype=F32), V(4, 4, 2, 2, 192, 128), V(4, 384, 128), V(3, 384, 128),
        V(4, 32, 128, dtype=F32), V(4, 32, 128, dtype=F32), V(4, 4, 2, 1, 128, dtype=F32), V(4, 32, 128, dtype=F32), V(512, 96),
        D(8), D(4), D(4),
        D(6), D(6), D(3), D(3), D(), D(), D(), D(), D(3), D(3), D(3), D(3), D(), D(),
        D(4), D(4), D(4), D(4), D(6), D(6), D(6), D(6), D(3), D(3), D(3), D(3),
        D(3), D(3), D(3), D(3), D(6), D(6), D(6), D(6), D(10), D(10),
        D(6), D(6), D(3), D(3), D(7), D(7), D(3), D(3),
    ]
    smem = pl.BlockSpec(memory_space=pltpu.SMEM)
    vmem = pl.BlockSpec(memory_space=pltpu.VMEM)
    where = pl.BlockSpec(memory_space=pl.ANY)
    return pl.pallas_call(
        kernel,
        out_shape=(
            pltpu.VMEM((384, 128), BF16),
            pltpu.VMEM((384, 128), BF16),
            pltpu.VMEM((128, 128), F32),
        ),
        in_specs=[where, where, smem] + [where] * 5,
        out_specs=(vmem, vmem, vmem),
        scratch_shapes=scratch,
        compiler_params=pltpu.CompilerParams(
            collective_id=0, has_side_effects=True, vmem_limit_bytes=56 * 2**20),
    )(tile_dest, tile_src, tile_count, source_of, features, weight, out_grad, tiles[0])


def solution(mesh):
    placed = (
        P(("row", "col"), None),
        P(),
        P("row", "col", None, None),
        P("row", "col"),
        P("row", "col"),
        P("row", "col"),
        P(("row", "col")),
        P(("row", "col"), None),
    )
    return jax.shard_map(
        local,
        mesh=mesh,
        in_specs=placed,
        out_specs=(P(("row", "col"), None), P(("row", "col"), None), P()),
        check_vma=False,
    )
```

```python
import functools
import math

import jax
import jax.numpy as jnp
from jax import lax
from jax.experimental import pallas as pl
from jax.experimental.pallas import tpu as pltpu
from jax.sharding import PartitionSpec as P

MESH = pl.DeviceIdType.MESH
F32 = jnp.float32
BF16 = jnp.bfloat16
UNROLL = 64


def mm(a, b):
    return jnp.dot(a, b, preferred_element_type=F32)


def sigmoid(v):
    return 1.0 / (1.0 + jnp.exp(-v))


def iota(shape, dim):
    return lax.broadcasted_iota(jnp.int32, shape, dim)


def kernel(
    dest_h, src_h, count_s, owner_h, feat_h, weight_h, grad_h, tiles_h,
    act_out, fg_out, wg_out,
    tiles, run, fall, weight, out_grad, dest_v, src_v, owner_v,
    dest_s, src_s, prevd_v, prevs_v, lastd_v, lasts_v, prevd_s, prevs_s, lastd_s, lasts_s,
    place, place_t, regroup, regroup_t, pick, pick_t,
    id_m, id_z, id_g, id_c,
    og_m, og_c, og_g, og_z,
    ac_m, ac_z, ac_g, ac_c,
    sx_out, sy_out, sx_in, sy_in, x_out, y_out, x_in, y_in, x2_out, y2_out, x2_in, y2_in,
    dgrad, gath, hg_out, hg_in, dw, dw_in, dw_all, spare,
    l_sem, t_sem, i_sem,
    f_s, f_r, idz_s, idz_r, idc_s, idc_r, ogc_s, ogc_r, ogz_s, ogz_r, acz_s, acz_r, acc_s, acc_r,
    sx_s, sx_r, sy_s, sy_r, rx_s, rx_r, ry_s, ry_r, rx2_s, rx2_r, ry2_s, ry2_r,
    ax_s, ax_r, ay_s, ay_r, gx_s, gx_r, gy_s, gy_r, as_s, as_r,
    hg_s, hg_r, wz_s, wz_r, wg_s, wg_r, wa_s, wa_r,
):
    r = lax.axis_index("row")
    c = lax.axis_index("col")
    x = c // 8
    y = (c // 2) % 4
    e = c % 2

    def at_chip(px, py):
        return {"row": r, "col": px * 8 + py * 2 + e}

    sibling = {"row": r, "col": x * 8 + y * 2 + (1 - e)}

    def send(src, dst, ss, rs, device):
        cp = pltpu.make_async_remote_copy(
            src_ref=src, dst_ref=dst, send_sem=ss, recv_sem=rs,
            device_id=device, device_id_type=MESH)
        cp.start()
        return cp

    def arrived(view, sem):
        pltpu.make_async_copy(view, view, sem).wait()

    def to_rows(src_of, dst, ss, rs):
        out = []
        for d in (2, 1, 3):
            to = lax.rem(r + d, 4)
            out.append(send(src_of(to), dst.at[r], ss.at[d - 1], rs.at[d - 1], {"row": to, "col": c}))
        return out

    def to_cols(src, dst, ss, rs):
        def one(d, carry):
            to = lax.rem(c + d, 32)
            send(src.at[to], dst.at[c], ss, rs, {"row": r, "col": to})
            return carry
        lax.fori_loop(1, 32, one, 0)

    def cols_done(src, dst, ss, rs):
        arrived(src.at[pl.ds(0, 31)], ss)
        arrived(dst.at[pl.ds(0, 31)], rs)

    def done(copies):
        for cp in copies:
            cp.wait()

    class Gather:
        def __init__(self, view, me, device, ss, rs):
            self.view, self.ss, self.rs = view, ss, rs
            self.right, self.left = lax.rem(me + 1, 4), lax.rem(me + 3, 4)
            self.to_right, self.to_left = device(self.right), device(self.left)
            self.copies = {}
            for n, half, device in ((0, 0, self.to_right), (2, 1, self.to_left), (1, 1, self.to_right), (3, 0, self.to_left)):
                self.go(n, view(me, half), device)

        def go(self, n, ref, device):
            self.copies[n] = send(ref, ref, self.ss.at[n], self.rs.at[n], device)

        def relay(self):
            self.copies[0].wait_recv()
            self.go(4, self.view(self.left, 0), self.to_right)
            self.copies[2].wait_recv()
            self.go(5, self.view(self.right, 1), self.to_left)

        def near(self):
            self.copies[1].wait_recv()
            self.copies[3].wait_recv()

        def far(self):
            self.copies[4].wait_recv()
            self.copies[5].wait_recv()

        def sent(self):
            for n in range(6):
                self.copies[n].wait_send()

    class Reduce:
        def __init__(self, out, into, half, me, device, ss, rs):
            self.out, self.into, self.half, self.me = out, into, half, me
            self.ss, self.rs = ss, rs
            self.right, self.left = lax.rem(me + 1, 4), lax.rem(me + 3, 4)
            self.across = lax.rem(me + 2, 4)
            self.to_right, self.to_left = device(self.right), device(self.left)
            self.copies = {}

        def go(self, n, pos, half, device):
            self.copies[n] = send(
                self.out.at[(pos,) + self.half(half)], self.into.at[n], self.ss.at[n], self.rs.at[n], device)

        def send_across(self):
            self.go(0, self.across, 0, self.to_right)
            self.go(2, self.across, 1, self.to_left)

        def send_right(self):
            self.go(1, self.right, 1, self.to_right)

        def send_left(self):
            self.go(3, self.left, 0, self.to_left)

        def relay(self):
            for n, pos, half, device in ((0, self.right, 0, self.to_right), (2, self.left, 1, self.to_left)):
                self.copies[n].wait_recv()
                at = (pos,) + self.half(half)
                self.out[at] = (self.out[at].astype(F32) + self.into[n].astype(F32)).astype(BF16)
                self.go(4 + n // 2, pos, half, device)

        def total(self, half):
            first, second = ((3, 4), (1, 5))[half]
            self.copies[first].wait_recv()
            own = self.out[(self.me,) + self.half(half)].astype(F32) + self.into[first].astype(F32)
            self.copies[second].wait_recv()
            return own + self.into[second].astype(F32)

        def sent(self):
            for n in range(6):
                self.copies[n].wait_send()

    barrier = pltpu.get_barrier_semaphore()

    def greet(d, carry):
        pl.semaphore_signal(barrier, inc=1, device_id={"row": r, "col": lax.rem(c + d, 32)}, device_id_type=MESH)
        return carry
    lax.fori_loop(1, 32, greet, 0)
    for d in range(1, 4):
        pl.semaphore_signal(barrier, inc=1, device_id={"row": lax.rem(r + d, 4), "col": c}, device_id_type=MESH)

    def load(n, src, dst):
        cp = pltpu.make_async_copy(src, dst, l_sem.at[n])
        cp.start()
        return cp

    feat_load = load(0, feat_h, fall.at[r])
    key_loads = [load(1, dest_h, dest_v), load(2, src_h, src_v), load(3, owner_h, owner_v)]
    scalar_loads = [load(4, dest_h, dest_s), load(5, src_h, src_s)]
    later_loads = [load(6, weight_h, weight), load(7, grad_h, out_grad)]
    tile_loads = [pltpu.make_async_copy(tiles_h.at[pl.ds(64 * k, 64)], tiles.at[pl.ds(64 * k, 64)], t_sem.at[k]) for k in range(4)]
    for cp in tile_loads:
        cp.start()
    feat_load.wait()
    done(key_loads)

    def wide(piece):
        return jnp.concatenate([piece] * 3, axis=1)

    source_of = owner_v[...].reshape(1, 384).astype(F32)
    owner = jnp.floor((source_of + 0.5) * (1.0 / 384.0))
    number = source_of - owner * 384.0
    owner_col = wide(jnp.broadcast_to(owner, (128, 384)).T)
    earlier = (owner_col == owner) & (iota((384, 384), 0) < iota((384, 384), 1))
    rank = jnp.sum(jnp.where(earlier, 1.0, 0.0), axis=0, keepdims=True)
    spot = owner * 3.0 + rank
    four = owner * 4.0 + rank
    four_col = jnp.broadcast_to(four, (128, 384)).T
    four_col = jnp.concatenate([four_col] * 4, axis=1)
    lanes = jnp.where(four_col == iota((384, 512), 1).astype(F32), 1.0, 0.0).astype(BF16)
    upper = jnp.floor(number * 0.5)
    parts = jnp.where(iota((16, 384), 0) == 0, upper, number - 2.0 * upper).astype(BF16)
    sent = mm(parts, lanes).astype(BF16)
    for k in range(4):
        id_m[k] = sent[:, k * 128:(k + 1) * 128]
    pl.semaphore_wait(barrier, 34)
    idz = to_rows(lambda to: id_m.at[to], id_z, idz_s, idz_r)
    id_z[r] = id_m[r]

    features = to_rows(lambda to: fall.at[r], fall, f_s, f_r)


    live = count_s[0, 0]

    def chains(key_v, prev_v, last_v, prev_s, last_s, n):
        key = key_v[...]
        col = jnp.broadcast_to(key, (128, 256)).T
        flipped = jnp.concatenate([col, col], axis=1)
        at = iota((256, 256), 0)
        before = jnp.where((flipped == key) & (at < iota((256, 256), 1)), at, -1)
        best = jnp.max(before, axis=0, keepdims=True)
        prev_v[...] = jnp.where(best < 0, 256, best)
        at = iota((256, 128), 0)
        named = jnp.where((col == iota((256, 128), 1)) & (at < live), at, -1)
        best = jnp.max(named, axis=0, keepdims=True)
        last_v[...] = jnp.where(best < 0, 256, best)
        return [pltpu.make_async_copy(prev_v, prev_s, i_sem.at[n]), pltpu.make_async_copy(last_v, last_s, i_sem.at[n + 1])]

    index_loads = chains(dest_v, prevd_v, lastd_v, prevd_s, lastd_s, 0) + chains(src_v, prevs_v, lasts_v, prevs_s, lasts_s, 2)
    for cp in index_loads:
        cp.start()

    row = iota((512, 128), 0)
    finds = jnp.where(iota((512, 128), 1) == (row >> 4) * 4 + (row & 3), 1.0, 0.0).astype(BF16)
    done(idz)
    found = lax.dot_general(finds, id_z[...].reshape(64, 128), (((1,), (1,)), ((), ())), preferred_element_type=F32)
    lane = iota((512, 64), 1) - ((iota((512, 64), 0) >> 2) & 3) * 16
    upper = jnp.sum(jnp.where(lane == 0, found, 0.0), axis=1, keepdims=True)
    lower = jnp.sum(jnp.where(lane == 1, found, 0.0), axis=1, keepdims=True)
    id_g[...] = jnp.where(iota((512, 128), 1) < 64, upper, lower).astype(BF16).reshape(32, 16, 128)
    to_cols(id_g, id_c, idc_s, idc_r)
    id_c[c] = id_g[c]

    run[256] = jnp.zeros((128, 128), F32)

    def spread(q, s):
        wanted = ((q >> 2) & 3) * 96 + (q >> 4) * 3 + (q & 3)
        return jnp.where(((q & 3) < 3) & (s == wanted), 1.0, 0.0).astype(BF16)

    regroup[...] = spread(iota((512, 384), 0), iota((512, 384), 1))
    row = iota((512, 96), 0)
    at_spare = ((row & 3) == 3) & (iota((512, 96), 1) == ((row >> 2) & 3) * 32 + (row >> 4))
    spare[...] = jnp.where(at_spare, 1.0, 0.0).astype(BF16)
    regroup_t[...] = spread(iota((384, 512), 1), iota((384, 512), 0))
    place[...] = jnp.where(iota((384, 384), 0).astype(F32) == spot, 1.0, 0.0).astype(BF16)
    spot_col = wide(jnp.broadcast_to(spot, (128, 384)).T)
    place_t[...] = jnp.where(spot_col == iota((384, 384), 1).astype(F32), 1.0, 0.0).astype(BF16)
    done(index_loads)
    done(scalar_loads)
    done(tile_loads)
    for cp in features:
        cp.wait_recv()

    blocks = fall.reshape(12, 128, 128)

    def forward(i, carry):
        for k in range(UNROLL):
            t = i * UNROLL + k
            run[t] = run[prevd_s[0, t]] + mm(tiles[t], blocks[src_s[0, t]])
        return carry
    lax.fori_loop(0, 256 // UNROLL, forward, 0)

    steps = (("x", 2), ("y", 2), ("x", 1), ("x", 3), ("y", 1), ("y", 3), ("x", 0), ("y", 0))

    def first_rows(chip, core):
        b = (chip * 2 + core) * 3
        return run[lastd_s[0, b]], run[lastd_s[0, b + 1], pl.ds(0, 64), :]

    def last_rows(chip, core):
        b = (chip * 2 + core) * 3
        return run[lastd_s[0, b + 1], pl.ds(64, 64), :], run[lastd_s[0, b + 2]]

    sib = {}
    for axis, d in steps:
        if axis == "x":
            g = lax.rem(x + d, 4)
            for k in range(4):
                rows0, rows1 = first_rows(g * 4 + k, 1 - e)
                sx_out[g, k, pl.ds(0, 128), :] = rows0.astype(BF16)
                sx_out[g, k, pl.ds(128, 64), :] = rows1.astype(BF16)
            sib[axis, d] = send(sx_out.at[g], sx_in.at[g], sx_s.at[d], sx_r.at[d], sibling)
        else:
            g = lax.rem(y + d, 4)
            for k in range(4):
                rows0, rows1 = last_rows(k * 4 + g, 1 - e)
                sy_out[g, k, pl.ds(0, 64), :] = rows0.astype(BF16)
                sy_out[g, k, pl.ds(64, 128), :] = rows1.astype(BF16)
            sib[axis, d] = send(sy_out.at[g], sy_in.at[g], sy_s.at[d], sy_r.at[d], sibling)

    done(later_loads)
    cols_done(id_g, id_c, idc_s, idc_r)
    numbers = id_c[...].reshape(512, 128).astype(F32)
    swapped = jnp.concatenate([numbers[:, 64:128], numbers[:, 0:64]], axis=1)
    low_lane = iota((512, 128), 1) < 64
    slot_id = 2.0 * jnp.where(low_lane, numbers, swapped) + jnp.where(low_lane, swapped, numbers)
    slot_id = jnp.where((iota((512, 128), 0) & 3) < 3, slot_id, -1.0)
    pick[...] = jnp.where(wide(slot_id) == iota((512, 384), 1).astype(F32), 1.0, 0.0).astype(BF16)
    og_m[...] = mm(pick[...], out_grad[...]).astype(BF16).reshape(32, 16, 128)
    to_cols(og_m, og_c, ogc_s, ogc_r)
    og_c[c] = og_m[c]

    def pair(half):
        return (pl.ds(2 * half, 2),)

    rx = Reduce(x_out, x_in, pair, x, lambda pos: at_chip(pos, y), rx_s, rx_r)
    ry = Reduce(y_out, y_in, pair, y, lambda pos: at_chip(x, pos), ry_s, ry_r)
    for axis, d in steps:
        sib[axis, d].wait_recv()
        if axis == "x":
            g = lax.rem(x + d, 4)
            for k in range(4):
                rows0, rows1 = first_rows(g * 4 + k, e)
                x_out[g, k, pl.ds(0, 128), :] = (rows0 + sx_in[g, k, pl.ds(0, 128), :].astype(F32)).astype(BF16)
                x_out[g, k, pl.ds(128, 64), :] = (rows1 + sx_in[g, k, pl.ds(128, 64), :].astype(F32)).astype(BF16)
        else:
            g = lax.rem(y + d, 4)
            for k in range(4):
                rows0, rows1 = last_rows(k * 4 + g, e)
                y_out[g, k, pl.ds(0, 64), :] = (rows0 + sy_in[g, k, pl.ds(0, 64), :].astype(F32)).astype(BF16)
                y_out[g, k, pl.ds(64, 128), :] = (rows1 + sy_in[g, k, pl.ds(64, 128), :].astype(F32)).astype(BF16)
        ring = rx if axis == "x" else ry
        if d == 2:
            ring.send_across()
        elif d == 1:
            ring.send_right()
        elif d == 3:
            ring.send_left()

    cols_done(og_m, og_c, ogc_s, ogc_r)
    og_g[...] = mm(regroup_t[...], og_c[...].reshape(512, 128)).astype(BF16).reshape(4, 96, 128)
    ogz = to_rows(lambda to: og_g.at[to], og_z, ogz_s, ogz_r)
    og_z[r] = og_g[r]

    rx.relay()
    ry.relay()

    slot_row = slot_id.T
    slot_row = jnp.concatenate([slot_row] * 3, axis=0)
    pick_t[...] = jnp.where(slot_row == iota((384, 512), 0).astype(F32), 1.0, 0.0).astype(BF16)

    rx2, ry2 = [], []
    for half in range(2):
        x2_out[pl.ds(2 * half, 2)] = rx.total(half).astype(BF16)
    for d in (2, 1, 3):
        py = lax.rem(y + d, 4)
        rx2.append(send(x2_out.at[py], x2_in.at[y], rx2_s.at[d - 1], rx2_r.at[d - 1], at_chip(x, py)))
    for half in range(2):
        y2_out[pl.ds(2 * half, 2)] = ry.total(half).astype(BF16)
    for d in (2, 1, 3):
        px = lax.rem(x + d, 4)
        ry2.append(send(y2_out.at[px], y2_in.at[x], ry2_s.at[d - 1], ry2_r.at[d - 1], at_chip(px, y)))

    done(ogz)
    dgrad[...] = mm(place_t[...], og_z[...].reshape(384, 128))
    for cp in features:
        cp.wait_send()

    done(rx2)
    top = x2_out[y].astype(F32)
    for d in range(1, 4):
        top += x2_in[lax.rem(y + d, 4)].astype(F32)
    done(ry2)
    low = y2_out[x].astype(F32)
    for d in range(1, 4):
        low += y2_in[lax.rem(x + d, 4)].astype(F32)
    sums = jnp.concatenate([top, low], axis=0)
    sums_high = sums.astype(BF16)
    sums_low = (sums - sums_high.astype(F32)).astype(BF16)
    pre = (mm(sums_high, weight[...]) + mm(sums_low, weight[...])).astype(BF16).astype(F32)
    sg = sigmoid(pre)
    grad = (dgrad[...] * (sg * (1.0 + pre * (1.0 - sg)))).astype(BF16).astype(F32)
    turned = [grad[j * 128:(j + 1) * 128].T.astype(BF16) for j in range(3)]
    gath[x, y, e, 0, pl.ds(0, 128), :] = turned[0]
    gath[x, y, e, 0, pl.ds(128, 64), :] = turned[1][0:64]
    gath[x, y, e, 1, pl.ds(0, 64), :] = turned[1][64:128]
    gath[x, y, e, 1, pl.ds(64, 128), :] = turned[2]

    ax, ay = [], []
    for d in (2, 1, 3):
        part = gath.at[x, y, e, 0]
        ax.append(send(part, part, ax_s.at[d - 1], ax_r.at[d - 1], at_chip(lax.rem(x + d, 4), y)))
        part = gath.at[x, y, e, 1]
        ay.append(send(part, part, ay_s.at[d - 1], ay_r.at[d - 1], at_chip(x, lax.rem(y + d, 4))))

    ac_m[...] = mm(place[...], (pre * sg).astype(BF16)).astype(BF16).reshape(4, 96, 128)
    acz = to_rows(lambda to: ac_m.at[to], ac_z, acz_s, acz_r)
    ac_z[r] = ac_m[r]
    term = jnp.zeros((128, 128), F32)
    for j in range(3):
        rows = slice(j * 128, (j + 1) * 128)
        term += mm(turned[j], sums_high[rows]) + mm(turned[j], sums_low[rows])
    dw[...] = term.T.reshape(4, 32, 128)
    wz = to_rows(lambda to: dw.at[to], dw_in, wz_s, wz_r)

    done(ax)
    by_y = Gather(lambda pos, half: gath.at[pl.ds(2 * half, 2), pos, e, 0], y, lambda pos: at_chip(x, pos), gy_s, gy_r)
    done(ay)
    by_x = Gather(lambda pos, half: gath.at[pos, pl.ds(2 * half, 2), e, 1], x, lambda pos: at_chip(pos, y), gx_s, gx_r)
    asib = []

    def share(n, part):
        asib.append(send(part, part, as_s.at[n], as_r.at[n], sibling))

    share(0, gath.at[:, y, e, 0])
    share(1, gath.at[x, :, e, 1])

    done(acz)
    done(wz)
    total = dw[r]
    for d in range(1, 4):
        total += dw_in[lax.rem(r + d, 4)]
    high = total.astype(BF16)
    rest = total - high.astype(F32)
    middle = rest.astype(BF16)
    low = (rest - middle.astype(F32)).astype(BF16)
    ac_g[...] = (mm(regroup[...], ac_z[...].reshape(384, 128)) + mm(spare[...], jnp.concatenate([high, middle, low], axis=0))
                 ).astype(BF16).reshape(32, 16, 128)
    to_cols(ac_g, ac_c, acc_s, acc_r)
    ac_c[c] = ac_g[c]

    by_y.relay()
    by_x.relay()
    by_y.near()
    share(2, gath.at[:, by_y.left, e, 0])
    share(3, gath.at[:, by_y.right, e, 0])
    by_x.near()
    share(4, gath.at[by_x.left, :, e, 1])
    share(5, gath.at[by_x.right, :, e, 1])

    for half in range(2):
        by_y.copies[4 + half].wait_recv()
        share(6 + half, by_y.view(lax.rem(y + 2, 4), half))
        by_x.copies[4 + half].wait_recv()
        share(8 + half, by_x.view(lax.rem(x + 2, 4), half))

    cols_done(ac_g, ac_c, acc_s, acc_r)
    came = ac_c[...].reshape(512, 128)
    act_out[...] = mm(pick_t[...], came).astype(BF16)
    ones = jnp.where((iota((16, 512), 1) & 3) == 3, 1.0, 0.0).astype(BF16)
    mine = mm(ones, came)[0:1] * (1.0 / math.sqrt(49152.0))
    dw_all[r, x, y, e] = mine
    w_copies = []
    for d in (2, 1, 3):
        part = dw_all.at[r, x, y, e]
        w_copies.append(send(part, part, wa_s.at[d - 1], wa_r.at[d - 1], {"row": lax.rem(r + d, 4), "col": c}))
    for cp in asib:
        cp.wait_recv()

    grads = gath.reshape(96, 128, 128)

    def backward(i, carry):
        for k in range(UNROLL):
            t = i * UNROLL + k
            run[t] = run[prevs_s[0, t]] + mm(grads[dest_s[0, t]], tiles[t])
        return carry
    lax.fori_loop(0, 128 // UNROLL, backward, 0)

    for cp in w_copies:
        cp.wait_recv()
    part = dw_all.at[:, x, y, e]
    w_copies.append(send(part, part, wg_s.at[0], wg_r.at[0], sibling))
    lax.fori_loop(128 // UNROLL, 256 // UNROLL, backward, 0)

    def finish(pos):
        for j in range(3):
            hg_out[pos, pl.ds(j * 128, 128), :] = run[lasts_s[0, pos * 3 + j]].astype(BF16)

    w_copies[3].wait_recv()
    for d in (2, 1, 3):
        part = dw_all.at[:, x, y]
        w_copies.append(send(part, part, wg_s.at[d], wg_r.at[d], at_chip(lax.rem(x + d, 4), y)))

    hgc = []
    for d in (2, 1, 3):
        to = lax.rem(r + d, 4)
        finish(to)
        hgc.append(send(hg_out.at[to], hg_in.at[d - 1], hg_s.at[d - 1], hg_r.at[d - 1], {"row": to, "col": c}))
    finish(r)

    for cp in w_copies[4:]:
        cp.wait_recv()
    for d in (2, 1, 3):
        part = dw_all.at[:, :, y]
        w_copies.append(send(part, part, wg_s.at[3 + d], wg_r.at[3 + d], at_chip(x, lax.rem(y + d, 4))))

    by_y.sent()
    by_x.sent()
    rx.sent()
    ry.sent()
    for cp in asib + list(sib.values()):
        cp.wait_send()
    total = hg_out[r].astype(F32)
    for n, d in ((1, 1), (2, 3), (0, 2)):
        hgc[n].wait_recv()
        total += hg_in[d - 1].astype(F32)
    hidden_grad = total.astype(BF16)
    for j in range(3):
        fg_out[pl.ds(j * 128, 128), :] = mm(weight[...], hidden_grad[j * 128:(j + 1) * 128]).T.astype(BF16)
    for cp in hgc + w_copies:
        cp.wait_send()
    for cp in w_copies[7:]:
        cp.wait_recv()
    wg_out[...] = dw_all[...].reshape(128, 128)


def local(features, weight, tiles, tile_dest, tile_src, tile_count, source_of, out_grad):
    def V(*shape, dtype=BF16):
        return pltpu.VMEM(shape, dtype)

    def D(*n):
        return pltpu.SemaphoreType.DMA(n) if n else pltpu.SemaphoreType.DMA

    I32 = jnp.int32
    scratch = [
        V(256, 128, 128), V(257, 128, 128, dtype=F32), V(4, 384, 128), V(128, 128), V(384, 128),
        V(1, 256, dtype=I32), V(1, 256, dtype=I32), V(384, dtype=I32),
        pltpu.SMEM((1, 256), I32), pltpu.SMEM((1, 256), I32),
        V(1, 256, dtype=I32), V(1, 256, dtype=I32), V(1, 128, dtype=I32), V(1, 128, dtype=I32),
        pltpu.SMEM((1, 256), I32), pltpu.SMEM((1, 256), I32), pltpu.SMEM((1, 128), I32), pltpu.SMEM((1, 128), I32),
        V(384, 384), V(384, 384), V(512, 384), V(384, 512), V(512, 384), V(384, 512),
        V(4, 16, 128), V(4, 16, 128), V(32, 16, 128), V(32, 16, 128),
        V(32, 16, 128), V(32, 16, 128), V(4, 96, 128), V(4, 96, 128),
        V(4, 96, 128), V(4, 96, 128), V(32, 16, 128), V(32, 16, 128),
        V(4, 4, 192, 128), V(4, 4, 192, 128), V(4, 4, 192, 128), V(4, 4, 192, 128),
        V(4, 4, 192, 128), V(4, 4, 192, 128), V(6, 2, 192, 128), V(6, 2, 192, 128),
        V(4, 192, 128), V(4, 192, 128), V(4, 192, 128), V(4, 192, 128),
        V(384, 128, dtype=F32), V(4, 4, 2, 2, 192, 128), V(4, 384, 128), V(3, 384, 128),
        V(4, 32, 128, dtype=F32), V(4, 32, 128, dtype=F32), V(4, 4, 4, 2, 1, 128, dtype=F32), V(512, 96),
        D(8), D(4), D(4),
        D(6), D(6), D(3), D(3), D(), D(), D(), D(), D(3), D(3), D(3), D(3), D(), D(),
        D(4), D(4), D(4), D(4), D(6), D(6), D(6), D(6), D(3), D(3), D(3), D(3),
        D(3), D(3), D(3), D(3), D(6), D(6), D(6), D(6), D(10), D(10),
        D(6), D(6), D(3), D(3), D(7), D(7), D(3), D(3),
    ]
    smem = pl.BlockSpec(memory_space=pltpu.SMEM)
    vmem = pl.BlockSpec(memory_space=pltpu.VMEM)
    where = pl.BlockSpec(memory_space=pl.ANY)
    return pl.pallas_call(
        kernel,
        out_shape=(
            pltpu.VMEM((384, 128), BF16),
            pltpu.VMEM((384, 128), BF16),
            pltpu.VMEM((128, 128), F32),
        ),
        in_specs=[where, where, smem] + [where] * 5,
        out_specs=(vmem, vmem, vmem),
        scratch_shapes=scratch,
        compiler_params=pltpu.CompilerParams(
            collective_id=0, has_side_effects=True, vmem_limit_bytes=56 * 2**20),
    )(tile_dest, tile_src, tile_count, source_of, features, weight, out_grad, tiles[0])


def solution(mesh):
    placed = (
        P(("row", "col"), None),
        P(),
        P("row", "col", None, None),
        P("row", "col"),
        P("row", "col"),
        P("row", "col"),
        P(("row", "col")),
        P(("row", "col"), None),
    )
    return jax.shard_map(
        local,
        mesh=mesh,
        in_specs=placed,
        out_specs=(P(("row", "col"), None), P(("row", "col"), None), P()),
        check_vma=False,
    )
```
